32 devices in a mesh: req: 4 (over y, core), exp: 8 (over z, x).
Axes of the slice: x: 2, y: 2, z: 4, core: 2. Of those that a mesh axis runs over, the one named last changes fastest.
Arguments:
- residual: bfloat16 [4160, 2048], P(('req', 'exp')), may hold values from -6 to 6
- prefill_qkv: bfloat16 [8, 3, 512, 2048], P('req', None, None, 'exp'), may hold values from -4.5 to 4.5
- decode_qkv: bfloat16 [64, 3, 2048], P('req', None, 'exp'), may hold values from -4.5 to 4.5
- cache_pool: bfloat16 [2, 496, 128, 2048], P(None, 'req', None, 'exp'), may hold values from -4.5 to 4.5
- page_table: int32 [64, 64], P('req'), may hold values from 0 to 123, as said below
- cache_len: int32 [64], P('req'), may hold values from 2 to 8192
- out_weight: bfloat16 [2048, 2048], P('exp'), may hold values from -0.125 to 0.125
- norm_gain: float32 [2048], replicated, may hold values from 0.1 to 1.9
- shared_gate_up: bfloat16 [2, 2048, 5632], P(None, None, 'exp'), may hold values from -0.125 to 0.125
- shared_down: bfloat16 [5632, 2048], P('exp'), may hold values from -0.078125 to 0.078125
- shared_gate: bfloat16 [2048], replicated, may hold values from -0.25 to 0.25
- routes: int32 [4160, 4], P(('req', 'exp')), may hold values from 0 to 31, all different within a row; in each aligned block of 130 rows (0 to 129, 130 to 259, ...) at most 32 rows name the same one
- route_weight: float32 [4160, 4], P(('req', 'exp')), may hold values from 0.1 to 0.5
- expert_gate_up: bfloat16 [32, 2, 2048, 1408], P(('req', 'exp')), may hold values from -0.125 to 0.125
- expert_down: bfloat16 [32, 1408, 2048], P(('req', 'exp')), may hold values from -0.15625 to 0.15625
Outputs:
- layer_out: bfloat16 [4160, 2048], P(('req', 'exp'))
The draws below stay inside these ranges and needn't reach their ends.
Inputs may be any that keep to these rules, and one draw needn't show every extreme that they name: `page_table`: for decode request i the first ceil(cache_len[i] / 128) entries name distinct pages among the requests of one req index and hold its cache in order; later entries name pages but are not read. `routes`: in the rows of one device (aligned blocks of 130 rows) no expert is named more than 32 times; a row names 4 different experts.
All inputs are finite; a program needn't handle non-finite values.
Results may differ from the reference program's by a relative error of at most 0.015.
Values may be sent and summed in bfloat16 or wider, within the bound.
A program may use at most 128 MiB of HBM per device.

```python
import math
import jax
import jax.numpy as jnp
import numpy as np
from jax import lax

D = 2048
HEADS = 16
HD = 128
FE = 1408
FS = 5632
TOPK = 4
SPAN = 512
PRE_DEV = 2
DEC_DEV = 16
PAGE = 128
MAXLEN = 8192
EXPERTS = 32
SPLIT = 1
FE_DEV = 1408
FS_DEV = 704
MAXPAGES = 64
SHORTPAGES = 4
PAGES_DEV = 124
T_DEV = 130
CAP = 32
PREFILL = 8
DECODE = 64
PAGES = 496
TOKENS = 4160
SHARDS = 32
N_REQ = 4
N_EXP = 8
DEVICES = 32


def shuffle_pages(page_key):
    return jax.random.permutation(page_key, PAGES_DEV)


def pick_pages(shuffled_row, slot_rows):
    return shuffled_row[slot_rows]


def pages_and_lengths(key):
    base_key = jax.random.fold_in(key, 7)
    first_key, second_key, third_key = jax.random.split(base_key, 3)
    long_slot = jax.random.randint(first_key, (N_REQ, 1), 0, DEC_DEV)
    short_len = jax.random.randint(second_key, (N_REQ, DEC_DEV), 2, SHORTPAGES * PAGE + 1)
    request_order = jnp.arange(DEC_DEV)[None, :]
    lengths = jnp.where(request_order == long_slot, MAXLEN, short_len)
    shuffled = jax.vmap(shuffle_pages)(jax.random.split(third_key, N_REQ))
    first_page = request_order * SHORTPAGES + (MAXPAGES - SHORTPAGES) * (request_order > long_slot).astype(jnp.int32)
    page_slots = (first_page[:, :, None] + jnp.arange(MAXPAGES)[None, None, :]) % PAGES_DEV
    page_rows = jax.vmap(pick_pages)(shuffled, page_slots)
    return (page_rows.reshape(DECODE, MAXPAGES).astype(jnp.int32), lengths.reshape(DECODE).astype(jnp.int32))


def base_values(key, shape):
    return jnp.clip(jax.random.normal(key, shape, jnp.float32), -4.0, 4.0)


def draw_prefill_qkv(key, part):
    values = base_values(jax.random.fold_in(key, 1), (PREFILL, 3, SPAN, D))
    return values.astype(jnp.bfloat16)


def draw_decode_qkv(key, part):
    values = base_values(jax.random.fold_in(key, 2), (DECODE, 3, D))
    return values.astype(jnp.bfloat16)


def draw_cache_pool(key, part):
    values = base_values(jax.random.fold_in(key, 4), (2, PAGES, PAGE, D))
    return values.astype(jnp.bfloat16)


def draw_page_table(key, part):
    return pages_and_lengths(key)[0]


def draw_cache_len(key, part):
    return pages_and_lengths(key)[1]


def steps_of(rng, dims, cuts, smallest, largest):
    loudness = 1.0
    for dim, parts in cuts:
        draws = jax.random.uniform(jax.random.fold_in(jax.random.fold_in(rng, 6), dim), (parts,), jnp.float32, smallest / len(cuts), largest / len(cuts))
        loudness = loudness * jnp.repeat(jnp.exp(draws), dims[dim] // parts).reshape((-1,) + (1,) * (len(dims) - 1 - dim))
    return loudness


def deal_out(key, own, number, rows, number_of, top, limit, lean):
    ranking = jax.random.permutation(key, number_of)
    heavy_load, ordinary = portions_of(number_of, rows * top, limit, lean, True), portions_of(number_of, rows * top, limit, lean, False)
    places = jnp.arange(number_of)

    def named(sizes, offset_by):
        used = int((sizes > 0).sum())
        fixed = max(1, used // 4)
        shifted = fixed + (places - fixed + offset_by * (used - fixed)) % max(1, number_of - fixed)
        return jnp.zeros((number_of,), jnp.int32).at[ranking[jnp.where(places < fixed, places, shifted)]].set(jnp.asarray(sizes, jnp.int32))

    sizes = jnp.where(number % 4 == 0, named(heavy_load, number // 4), named(ordinary, number - number // 4 - 1))
    mixed = jax.random.permutation(jax.random.fold_in(own, 3), number_of)
    source_of, receiver = mixed[0:number_of // 2 * 2:2], mixed[1:number_of // 2 * 2:2]
    margin = jnp.minimum(sizes[source_of] - 1, limit - sizes[receiver]) // 2
    margin = jnp.where((source_of == ranking[0]) | (receiver == ranking[0]) | (sizes[receiver] == 0), 0, jnp.maximum(margin, 0))
    shifted = jax.random.randint(jax.random.fold_in(own, 4), (number_of // 2,), 0, 1 << 20) % (margin + 1)
    sizes = sizes.at[source_of].add(-shifted).at[receiver].add(shifted)
    items = jnp.searchsorted(jnp.cumsum(sizes), jnp.arange(rows * top), side="right").astype(jnp.int32)
    grid = items.reshape(top, rows).T
    grid = grid[jax.random.permutation(jax.random.fold_in(own, 1), rows)]
    offset_by = jax.random.randint(jax.random.fold_in(own, 2), (rows, 1), 0, top)
    return jnp.take_along_axis(grid, (jnp.arange(top)[None, :] + offset_by) % top, axis=1)


def portions_of(count, total, reach, skew, full):
    portions = [(1 << 20) // math.isqrt(standing ** skew) + 1 for standing in range(1, count + 1)]
    largest = reach if full else min(reach, max(-(-total // count), total * portions[0] // sum(portions)))
    least = 1 if total - largest >= count - 1 else 0
    counts, rest = [largest] + [least] * (count - 1), total - largest - least * (count - 1)
    while rest > 0:
        movable = [i for i in range(1, count) if counts[i] < largest] or [i for i in range(1, count) if counts[i] < reach]
        mass, remaining = sum([portions[i] for i in movable]), rest
        for i in movable:
            extra = min(reach - counts[i], max(1, remaining * portions[i] // mass), rest)
            counts[i] = counts[i] + extra
            rest = rest - extra
    return np.array(counts)


def normal_values(stream_key, shape, spread, limit, shards=(), held_as=jnp.bfloat16):
    result = jax.random.normal(stream_key, shape, jnp.float32) * spread
    if len(shards) > 0:
        result = steps_of(stream_key, shape, shards, -0.22, 0.18) * result
    return jnp.clip(result, min=-limit, max=limit).astype(held_as)


def setup_inputs(seed: int = 0) -> dict:
    key_list = jax.random.split(jax.random.key(seed), 16)
    residual = normal_values(key_list[0], (TOKENS, D), 1.0, 6.0, ((0, 32),))
    prefill_qkv = draw_prefill_qkv(jax.random.fold_in(key_list[15], 71), 0)
    decode_qkv = draw_decode_qkv(jax.random.fold_in(key_list[15], 71), 0)
    cache_pool = draw_cache_pool(jax.random.fold_in(key_list[15], 71), 0)
    page_table = draw_page_table(jax.random.fold_in(key_list[15], 71), 0)
    cache_len = draw_cache_len(jax.random.fold_in(key_list[15], 71), 0)
    out_weight = normal_values(key_list[6], (D, D), D ** -0.5, 0.125, ((0, 8),))
    norm_gain = jnp.clip(1.0 + 0.18 * jax.random.normal(key_list[7], (D,), jnp.float32), 0.1, 1.9)
    shared_gate_up = normal_values(key_list[8], (2, D, FS), D ** -0.5, 0.125, ((2, 8),))
    shared_down = normal_values(key_list[9], (FS, D), FS ** -0.5, 0.078125, ((0, 8),))
    shared_gate = normal_values(key_list[10], (D,), (D // 4) ** -0.5, 0.25)
    routes_keys = jax.random.split(jax.random.fold_in(key_list[11], 1), TOKENS // T_DEV)
    routes_turns = jax.random.permutation(jax.random.fold_in(key_list[11], 3), TOKENS // T_DEV)
    routes = jax.vmap(lambda own, number: deal_out(jax.random.fold_in(key_list[11], 2), own, number, T_DEV, EXPERTS, TOPK, CAP, 2))(routes_keys, routes_turns).reshape((TOKENS, TOPK))
    route_weight = jnp.clip(0.1 + 0.4 * jax.random.uniform(key_list[12], (TOKENS, TOPK), jnp.float32) ** steps_of(key_list[12], (TOKENS, TOPK), ((0, 32),), -0.2, 0.2), 0.1, 0.5)
    expert_gate_up = normal_values(key_list[13], (SHARDS, 2, D, FE_DEV), D ** -0.5, 0.125, ((0, 32),))
    expert_down = normal_values(key_list[14], (SHARDS, FE_DEV, D), FE ** -0.5, 0.15625, ((0, 32),))
    return dict(residual=residual, prefill_qkv=prefill_qkv, decode_qkv=decode_qkv, cache_pool=cache_pool, page_table=page_table, cache_len=cache_len, out_weight=out_weight, norm_gain=norm_gain, shared_gate_up=shared_gate_up, shared_down=shared_down, shared_gate=shared_gate, routes=routes, route_weight=route_weight, expert_gate_up=expert_gate_up, expert_down=expert_down)


NEG_FILL = -1e+30

def masked_weights(scores, allowed):
    masked = jnp.where(allowed, scores, NEG_FILL)
    highest = lax.optimization_barrier(jnp.max(masked, axis=-1, keepdims=True))
    raised = jnp.where(allowed, jnp.exp(masked - highest), 0.0)
    return (raised / lax.optimization_barrier(jnp.sum(raised, axis=-1, keepdims=True))).astype(jnp.bfloat16)

def reference(residual, prefill_qkv, decode_qkv, cache_pool, page_table, cache_len, out_weight, norm_gain, shared_gate_up, shared_down, shared_gate, routes, route_weight, expert_gate_up, expert_down):
    scaling = HD ** (-0.5)

    def prefill_one(span_qkv):
        split_qkv = span_qkv.reshape(3, SPAN, HEADS, HD).astype(jnp.float32)
        scores = jnp.einsum('qhd,khd->hqk', split_qkv[0], split_qkv[1]) * scaling
        causal = jnp.arange(SPAN)[:, None] >= jnp.arange(SPAN)[None, :]
        weights = masked_weights(scores, causal[None])
        mixed_rows = jnp.einsum('hqk,khd->qhd', weights.astype(jnp.float32), split_qkv[2])
        return mixed_rows.reshape(SPAN, D).astype(jnp.bfloat16)

    def decode_one(operands):
        request_qkv, page_rows, length, position = operands
        device_row = position // DEC_DEV
        page_data = jnp.take(cache_pool, (device_row * PAGES_DEV + page_rows).astype(jnp.int32), axis=1)
        cache_keys = page_data[0].reshape(MAXLEN, HEADS, HD).astype(jnp.float32)
        cache_values = page_data[1].reshape(MAXLEN, HEADS, HD).astype(jnp.float32)
        query_row = request_qkv[0].reshape(HEADS, HD).astype(jnp.float32)
        own_key = request_qkv[1].reshape(HEADS, HD).astype(jnp.float32)
        own_value = request_qkv[2].reshape(HEADS, HD).astype(jnp.float32)
        cached = jnp.einsum('hd,thd->ht', query_row, cache_keys) * scaling
        own_score = lax.optimization_barrier(jnp.sum(query_row * own_key, axis=-1, keepdims=True)) * scaling
        joined = jnp.concatenate([cached, own_score], axis=1)
        live = jnp.arange(MAXLEN) < length
        allowed = jnp.concatenate([jnp.broadcast_to(live[None, :], (HEADS, MAXLEN)), jnp.ones((HEADS, 1), bool)], axis=1)
        weights = masked_weights(joined, allowed)
        mixed_rows = jnp.einsum('ht,thd->hd', weights[:, :MAXLEN].astype(jnp.float32), cache_values)
        mixed_rows = mixed_rows + weights[:, MAXLEN:].astype(jnp.float32) * own_value
        return mixed_rows.reshape(D).astype(jnp.bfloat16)
    prefill_out = lax.map(prefill_one, prefill_qkv)
    decode_out = lax.map(decode_one, (decode_qkv, page_table, cache_len, jnp.arange(DECODE).astype(jnp.int32)))
    attended = jnp.concatenate([prefill_out.reshape(N_REQ, PRE_DEV * SPAN, D), decode_out.reshape(N_REQ, DEC_DEV, D)], axis=1).reshape(TOKENS, D)
    projected = jnp.dot(attended, out_weight, preferred_element_type=jnp.float32)
    stream = lax.optimization_barrier((residual.astype(jnp.float32) + projected).astype(jnp.bfloat16))
    stream_wide = stream.astype(jnp.float32)
    normed = (stream_wide * lax.rsqrt(lax.optimization_barrier(jnp.mean(stream_wide * stream_wide, axis=-1, keepdims=True)) + 1e-06) * norm_gain).astype(jnp.bfloat16)
    gate_part = jnp.dot(normed, shared_gate_up[0], preferred_element_type=jnp.float32)
    up_part = jnp.dot(normed, shared_gate_up[1], preferred_element_type=jnp.float32)
    shared_hidden = (jax.nn.silu(gate_part) * up_part).astype(jnp.bfloat16)
    shared_out = jnp.zeros((TOKENS, D), jnp.float32)
    for block_index in range(N_EXP):
        lower = block_index * FS_DEV
        partial_value = jnp.dot(shared_hidden[:, lower:lower + FS_DEV], shared_down[lower:lower + FS_DEV], preferred_element_type=jnp.float32).astype(jnp.bfloat16)
        shared_out = shared_out + lax.optimization_barrier(partial_value).astype(jnp.float32)
    shared_scale = jax.nn.sigmoid(jnp.dot(normed, shared_gate, preferred_element_type=jnp.float32))
    flat_routes = routes.reshape(-1)
    flat_weights = route_weight.reshape(-1)
    token_ids = (jnp.arange(TOKENS * TOPK) // TOPK).astype(jnp.int32)
    slot_total = DEVICES * CAP

    def one_expert(running, operands):
        expert_id, gate_up, down_rows = operands
        hit_mask = flat_routes == expert_id
        slot_rank = jnp.cumsum(hit_mask.astype(jnp.int32)) - 1
        target = jnp.where(hit_mask, slot_rank, slot_total).astype(jnp.int32)
        slot_token = jnp.zeros((slot_total,), jnp.int32).at[target].set(token_ids, mode='drop')
        slot_weight = jnp.zeros((slot_total,), jnp.float32).at[target].set(flat_weights, mode='drop')
        gathered = normed[slot_token]
        expert_out = jnp.zeros((slot_total, D), jnp.float32)
        for shard_index in range(SPLIT):
            expert_gate = jnp.dot(gathered, gate_up[shard_index, 0], preferred_element_type=jnp.float32)
            expert_up = jnp.dot(gathered, gate_up[shard_index, 1], preferred_element_type=jnp.float32)
            hidden = (jax.nn.silu(expert_gate) * expert_up).astype(jnp.bfloat16)
            part_out = jnp.dot(hidden, down_rows[shard_index], preferred_element_type=jnp.float32).astype(jnp.bfloat16)
            expert_out = expert_out + lax.optimization_barrier(part_out).astype(jnp.float32)
        running = running.at[slot_token].add(slot_weight[:, None] * expert_out)
        return (running, expert_id)
    scanned = lax.scan(one_expert, jnp.zeros((TOKENS, D), jnp.float32), (jnp.arange(EXPERTS).astype(jnp.int32), expert_gate_up.reshape(EXPERTS, SPLIT, 2, D, FE_DEV), expert_down.reshape(EXPERTS, SPLIT, FE_DEV, D)))
    routed = scanned[0]
    layer_out = stream_wide + routed + shared_scale[:, None] * shared_out
    return layer_out.astype(jnp.bfloat16)
```

```python
import functools

import jax
import jax.numpy as jnp
from jax import lax
from jax.experimental import pallas as pl
from jax.experimental.pallas import tpu as pltpu
from jax.sharding import PartitionSpec as P

HD = 128
EXP_COL = 4
ROW_TILE = 16


NEG_FILL = -1e30
ROWS_BY_ROWS = (((1,), (1,)), ((), ()))


def attention_kernel(
    heads, q_ref, k_ref, v_ref, dq_ref, dk_ref, dv_ref, code_ref, ck_ref, cv_ref, out_ref,
    high_ref, sum_ref, acc_ref,
):
    step = pl.program_id(0)
    scaling = HD ** (-0.5)
    span_len = q_ref.shape[2]
    requests, width = dq_ref.shape
    rows = heads * requests

    query, keys, values = (q_ref[0, 0], k_ref[0, 0], v_ref[0, 0])
    half = span_len // 2
    base = pl.multiple_of((step // heads) * span_len, span_len)
    lane = pl.multiple_of((step % heads) * HD, HD)
    for lower, upper in ((0, half), (half, span_len)):
        scores = lax.dot_general(
            query[lower:upper], keys[:upper], ROWS_BY_ROWS, preferred_element_type=jnp.float32
        ) * scaling
        row = lax.broadcasted_iota(jnp.int32, scores.shape, 0) + lower
        column = lax.broadcasted_iota(jnp.int32, scores.shape, 1)
        scores = jnp.where(row >= column, scores, NEG_FILL)
        raised = jnp.exp(scores - jnp.max(scores, axis=-1, keepdims=True))
        total = jnp.sum(raised, axis=-1, keepdims=True)
        mixed = jnp.dot(
            raised.astype(jnp.bfloat16), values[:upper], preferred_element_type=jnp.float32
        )
        out_ref[pl.ds(base + lower, upper - lower), pl.ds(lane, HD)] = (mixed / total).astype(
            out_ref.dtype
        )

    head_of = lax.broadcasted_iota(jnp.int32, (rows, width), 0) // requests
    lane_head = lax.broadcasted_iota(jnp.int32, (rows, width), 1) // HD
    queries = jnp.where(
        head_of == lane_head,
        jnp.concatenate([dq_ref[...].astype(jnp.float32)] * heads, axis=0),
        0.0,
    )

    @pl.when(step == 0)
    def _():
        own = jnp.concatenate([dk_ref[...].astype(jnp.float32)] * heads, axis=0)
        high_ref[...] = jnp.sum(queries * own, axis=-1, keepdims=True) * scaling
        sum_ref[...] = jnp.ones_like(sum_ref)
        acc_ref[...] = jnp.concatenate([dv_ref[...].astype(jnp.float32)] * heads, axis=0)

    scores = lax.dot_general(
        queries.astype(jnp.bfloat16), ck_ref[0], ROWS_BY_ROWS, preferred_element_type=jnp.float32
    ) * scaling
    request = lax.broadcasted_iota(jnp.int32, scores.shape, 0) % requests
    allowed = request == code_ref[...]
    scores = jnp.where(allowed, scores, NEG_FILL)
    before = high_ref[...]
    after = jnp.maximum(before, jnp.max(scores, axis=-1, keepdims=True))
    raised = jnp.where(allowed, jnp.exp(scores - after), 0.0)
    fade = jnp.exp(before - after)
    high_ref[...] = after
    sum_ref[...] = sum_ref[...] * fade + jnp.sum(raised, axis=-1, keepdims=True)
    acc_ref[...] = acc_ref[...] * fade + jnp.dot(
        raised.astype(jnp.bfloat16), cv_ref[0], preferred_element_type=jnp.float32
    )

    @pl.when(step == pl.num_programs(0) - 1)
    def _():
        mixed = acc_ref[...] / sum_ref[...]
        first = out_ref.shape[0] - requests
        for head in range(heads):
            lanes = slice(head * HD, (head + 1) * HD)
            out_ref[first:, lanes] = mixed[
                head * requests : (head + 1) * requests, lanes
            ].astype(out_ref.dtype)


def attend(prefill_qkv, decode_qkv, cache_pool, page_table, cache_len):
    spans, _, span_len, width = prefill_qkv.shape
    requests = decode_qkv.shape[0]
    heads = width // HD
    steps = spans * heads
    pool_pages, page_len = (cache_pool.shape[1], cache_pool.shape[2])
    max_pages = page_table.shape[1]
    chunk = pool_pages // steps * page_len
    order = jnp.arange(max_pages, dtype=jnp.int32)
    left = cache_len[:, None] - order[None, :] * page_len
    held = (page_table[None] == jnp.arange(pool_pages, dtype=jnp.int32)[:, None, None]) & (
        left > 0
    )[None]
    owner = jnp.max(
        jnp.where(held, jnp.arange(requests, dtype=jnp.int32)[None, :, None], -1), axis=(1, 2)
    )
    valid = jnp.max(jnp.where(held, left[None], 0), axis=(1, 2))
    code = jnp.where(
        jnp.arange(page_len, dtype=jnp.int32)[None, :] < valid[:, None], owner[:, None], -1
    ).reshape(1, pool_pages * page_len)
    pool = cache_pool.reshape(2, pool_pages * page_len, width)
    whole = pl.BlockSpec((requests, width), lambda g: (0, 0))
    part = [
        pl.BlockSpec((1, 1, span_len, HD), functools.partial(lambda j, g: (g // heads, j, 0, g % heads), j))
        for j in range(3)
    ]
    out_rows = spans * span_len + requests
    return pl.pallas_call(
        functools.partial(attention_kernel, heads),
        grid=(steps,),
        in_specs=part
        + [whole] * 3
        + [
            pl.BlockSpec((1, chunk), lambda g: (0, g)),
            pl.BlockSpec((1, chunk, width), lambda g: (0, g, 0)),
            pl.BlockSpec((1, chunk, width), lambda g: (1, g, 0)),
        ],
        out_specs=pl.BlockSpec((out_rows, width), lambda g: (0, 0)),
        out_shape=jax.ShapeDtypeStruct((out_rows, width), jnp.bfloat16),
        scratch_shapes=[
            pltpu.VMEM((heads * requests, 1), jnp.float32),
            pltpu.VMEM((heads * requests, 1), jnp.float32),
            pltpu.VMEM((heads * requests, width), jnp.float32),
        ],
        compiler_params=pltpu.CompilerParams(vmem_limit_bytes=40 * 2**20),
        cost_estimate=pl.CostEstimate(
            flops=2 * 10**9, bytes_accessed=2 * pool.size + 2 * prefill_qkv.size, transcendentals=2 * 10**6
        ),
    )(
        prefill_qkv, prefill_qkv, prefill_qkv,
        decode_qkv[:, 0], decode_qkv[:, 1], decode_qkv[:, 2],
        code, pool, pool,
    )


LINE = 4
MESH = pl.DeviceIdType.MESH


def greet(place, line, groups, columns):
    outer, inner = place
    long, short = line
    barrier = pltpu.get_barrier_semaphore()
    count = jnp.int32(0)
    for ok, target in (
        (outer > 0, (outer - 1) * short + inner),
        (outer < long - 1, (outer + 1) * short + inner),
        (inner > 0, outer * short + inner - 1),
        (inner < short - 1, outer * short + inner + 1),
    ):
        @pl.when(ok)
        def _():
            pl.semaphore_signal(barrier, inc=1, device_id={"exp": target}, device_id_type=MESH)

        count = count + ok.astype(jnp.int32)
    if columns > 1:
        me = lax.axis_index("req")
        for k in range(1, columns):
            pl.semaphore_signal(
                barrier, inc=1, device_id={"req": (me + k) % columns}, device_id_type=MESH
            )
        count = count + (columns - 1)
    pl.semaphore_wait(barrier, count)


def visit(place, long, farthest_first, body):
    outer = place[0]
    distances = range(long - 1, -1, -1) if farthest_first else range(long)
    for distance in distances:
        @pl.when(outer + distance < long)
        def _():
            body(outer + distance, distance, 0)

        if distance > 0:
            @pl.when(outer - distance >= 0)
            def _():
                body(outer - distance, distance, 1)


def reduce_scatter(place, line, part, fill, column, rin, rout, total, sems):
    outer, inner = place
    long, short = line
    isend, irecv, osend, orecv = sems

    def inner_copy(way, o, i, relay):
        target = outer * short + inner + (1 if way == 0 else -1)
        return pltpu.make_async_remote_copy(
            src_ref=(rin.at[way, o, i] if relay else part.at[o, i]),
            dst_ref=rin.at[way, o, i],
            send_sem=isend.at[way, o, i],
            recv_sem=irecv.at[way, o, i],
            device_id={"exp": target},
            device_id_type=MESH,
        )

    def outer_copy(way, o):
        target = (outer + (1 if way == 0 else -1)) * short + inner
        return pltpu.make_async_remote_copy(
            src_ref=column.at[o],
            dst_ref=rout.at[way, o],
            send_sem=osend.at[way, o],
            recv_sem=orecv.at[way, o],
            device_id={"exp": target},
            device_id_type=MESH,
        )

    def first(o, distance, side):
        fill(o)
        for way in (0, 1):
            for gap in range(short - 1, 0, -1):
                i = inner + gap if way == 0 else inner - gap
                ok = (i < short) if way == 0 else (i >= 0)
                behind = (inner > 0) if way == 0 else (inner < short - 1)
                if short == 2:
                    @pl.when(ok)
                    def _():
                        inner_copy(way, o, i, False).start()
                else:
                    @pl.when(ok & jnp.logical_not(behind))
                    def _():
                        inner_copy(way, o, i, False).start()

    visit(place, long, True, first)

    def second(o, distance, side):
        if short > 2:
            for way in (0, 1):
                for gap in range(short - 1, 0, -1):
                    i = inner + gap if way == 0 else inner - gap
                    ok = (i < short) if way == 0 else (i >= 0)
                    behind = (inner > 0) if way == 0 else (inner < short - 1)

                    @pl.when(ok & behind)
                    def _():
                        inner_copy(way, o, i, True).wait_recv()
                        rin[way, o, i] = (
                            rin[way, o, i].astype(jnp.float32) + part[o, i].astype(jnp.float32)
                        ).astype(jnp.bfloat16)
                        inner_copy(way, o, i, True).start()

        total[...] = part[o, inner].astype(jnp.float32)
        for way, behind in ((0, inner > 0), (1, inner < short - 1)):
            @pl.when(behind)
            def _():
                inner_copy(way, o, inner, False).wait_recv()
                total[...] += rin[way, o, inner].astype(jnp.float32)

        for way, behind in ((0, outer > 0), (1, outer < long - 1)):
            if distance == 0 or way == side:
                @pl.when(behind)
                def _():
                    outer_copy(way, o).wait_recv()
                    total[...] += rout[way, o].astype(jnp.float32)

        if distance > 0:
            column[o] = total[...].astype(jnp.bfloat16)
            outer_copy(side, o).start()

    visit(place, long, True, second)

    def finish():
        for o in range(long):
            for i in range(short):
                @pl.when(inner < i)
                def _():
                    inner_copy(0, o, i, False).wait_send()

                @pl.when(inner > i)
                def _():
                    inner_copy(1, o, i, False).wait_send()

            @pl.when(outer < o)
            def _():
                outer_copy(0, o).wait_send()

            @pl.when(outer > o)
            def _():
                outer_copy(1, o).wait_send()

    return finish


def front_kernel(
    line, columns, att_ref, w_ref, res_ref, gain_ref, sel_ref, stream_ref, all_ref, arr_ref,
    part, column, rin, rout, total, pack, isend, irecv, osend, orecv, asend, arecv, ysend, yrecv,
):
    long, short = line
    groups = long * short
    exp = lax.axis_index("exp")
    me = lax.axis_index("req")
    place = (exp // short, exp % short)
    outer, inner = place
    greet(place, line, groups, columns)

    def fill(o):
        for i in range(short):
            part[o, i] = jnp.dot(
                att_ref[o, i], w_ref[...], preferred_element_type=jnp.float32
            ).astype(jnp.bfloat16)

    finish = reduce_scatter(
        place, line, part, fill, column, rin, rout, total, (isend, irecv, osend, orecv)
    )
    stream = (res_ref[...].astype(jnp.float32) + total[...]).astype(jnp.bfloat16)
    stream_ref[...] = stream
    wide = stream.astype(jnp.float32)
    all_ref[outer, inner] = (
        wide
        * lax.rsqrt(jnp.mean(wide * wide, axis=-1, keepdims=True) + 1e-06)
        * gain_ref[...]
    ).astype(jnp.bfloat16)

    def pass_on(way, o, i):
        target = exp + (short, -short, 1, -1)[way]
        return pltpu.make_async_remote_copy(
            src_ref=all_ref.at[o, i],
            dst_ref=all_ref.at[o, i],
            send_sem=asend.at[way, o, i],
            recv_sem=arecv.at[o, i],
            device_id={"exp": target},
            device_id_type=MESH,
        )

    def to_column(k, o, i):
        target = (me + k) % columns
        return pltpu.make_async_remote_copy(
            src_ref=pack.at[o, i, target],
            dst_ref=arr_ref.at[me, o, i],
            send_sem=ysend.at[k, o, i],
            recv_sem=yrecv.at[k, o, i],
            device_id={"req": target},
            device_id_type=MESH,
        )

    def dispatch(o, i):
        rows = jnp.dot(
            sel_ref[o, i], all_ref[o, i], preferred_element_type=jnp.float32
        ).astype(jnp.bfloat16)
        pack[o, i] = rows.reshape(pack.shape[2:])
        for k in range(1, columns):
            to_column(k, o, i).start()
        arr_ref[me, o, i] = pack[o, i, me]

    def spread(o, distance, side):
        if distance > 0:
            pass_on(0, o, inner).wait_recv()
        for way, ahead in ((0, outer < long - 1), (1, outer > 0)):
            if distance == 0 or way == 1 - side:
                @pl.when(ahead)
                def _():
                    pass_on(way, o, inner).start()
        for way, ahead in ((2, inner < short - 1), (3, inner > 0)):
            @pl.when(ahead)
            def _():
                pass_on(way, o, inner).start()
        dispatch(o, inner)

    def across(o, distance, side):
        for gap in range(1, short):
            for way, i, ok, ahead in (
                (2, inner - gap, inner - gap >= 0, inner < short - 1),
                (3, inner + gap, inner + gap < short, inner > 0),
            ):
                @pl.when(ok)
                def _():
                    pass_on(way, o, i).wait_recv()
                    if short > 2:
                        @pl.when(ahead)
                        def _():
                            pass_on(way, o, i).start()
                    dispatch(o, i)

    for step in range(long + 1):
        if step < long:
            near(place, long, step, spread)
        if step > 0:
            near(place, long, step - 1, across)

    finish()
    for o in range(long):
        for i in range(short):
            at_line = inner == i
            @pl.when(at_line & (outer >= o) & (outer < long - 1))
            def _():
                pass_on(0, o, i).wait_send()

            @pl.when(at_line & (outer <= o) & (outer > 0))
            def _():
                pass_on(1, o, i).wait_send()

            @pl.when((inner >= i) & (inner < short - 1))
            def _():
                pass_on(2, o, i).wait_send()

            @pl.when((inner <= i) & (inner > 0))
            def _():
                pass_on(3, o, i).wait_send()

            for k in range(1, columns):
                to_column(k, o, i).wait_send()
                to_column(k, o, i).wait_recv()


def near(place, long, distance, body):
    outer = place[0]

    @pl.when(outer + distance < long)
    def _():
        body(outer + distance, distance, 0)

    if distance > 0:
        @pl.when(outer - distance >= 0)
        def _():
            body(outer - distance, distance, 1)


def front(attended, out_weight, residual, norm_gain, select, line, columns):
    long, short = line
    tokens, width = residual.shape
    depth = out_weight.shape[0]
    rows = select.shape[2] // columns
    dma = pltpu.SemaphoreType.DMA
    block = (long, short, tokens, width)
    vmem = pl.BlockSpec(memory_space=pltpu.VMEM)
    bf16 = jnp.bfloat16
    return pl.pallas_call(
        functools.partial(front_kernel, line, columns),
        out_shape=(
            jax.ShapeDtypeStruct((tokens, width), bf16),
            jax.ShapeDtypeStruct(block, bf16),
            jax.ShapeDtypeStruct((columns, long, short, rows, width), bf16),
        ),
        in_specs=[vmem] * 5,
        out_specs=(vmem, vmem, vmem),
        scratch_shapes=[
            pltpu.VMEM(block, bf16),
            pltpu.VMEM((long, tokens, width), bf16),
            pltpu.VMEM((2,) + block, bf16),
            pltpu.VMEM((2, long, tokens, width), bf16),
            pltpu.VMEM((tokens, width), jnp.float32),
            pltpu.VMEM((long, short, columns, rows, width), bf16),
            dma((2, long, short)),
            dma((2, long, short)),
            dma((2, long)),
            dma((2, long)),
            dma((4, long, short)),
            dma((long, short)),
            dma((columns, long, short)),
            dma((columns, long, short)),
        ],
        compiler_params=pltpu.CompilerParams(
            collective_id=0, has_side_effects=True, vmem_limit_bytes=56 * 2**20
        ),
        cost_estimate=pl.CostEstimate(
            flops=4 * 10**9, bytes_accessed=2 * 10**7, transcendentals=0
        ),
    )(
        attended.reshape(long, short, tokens, depth), out_weight, residual,
        norm_gain.reshape(1, width), select,
    )


def back_kernel(
    line, part_ref, stream_ref, out_ref, column, rin, rout, total, isend, irecv, osend, orecv
):
    exp = lax.axis_index("exp")
    place = (exp // line[1], exp % line[1])
    greet(place, line, line[0] * line[1], 1)
    finish = reduce_scatter(
        place, line, part_ref, lambda o: None, column, rin, rout, total,
        (isend, irecv, osend, orecv),
    )
    out_ref[...] = (stream_ref[...].astype(jnp.float32) + total[...]).astype(jnp.bfloat16)
    finish()


def back(partials, stream, line):
    long, short = line
    tokens, width = stream.shape
    dma = pltpu.SemaphoreType.DMA
    block = (long, short, tokens, width)
    vmem = pl.BlockSpec(memory_space=pltpu.VMEM)
    bf16 = jnp.bfloat16
    return pl.pallas_call(
        functools.partial(back_kernel, line),
        out_shape=jax.ShapeDtypeStruct((tokens, width), bf16),
        in_specs=[vmem] * 2,
        out_specs=vmem,
        scratch_shapes=[
            pltpu.VMEM((long, tokens, width), bf16),
            pltpu.VMEM((2,) + block, bf16),
            pltpu.VMEM((2, long, tokens, width), bf16),
            pltpu.VMEM((tokens, width), jnp.float32),
            dma((2, long, short)),
            dma((2, long, short)),
            dma((2, long)),
            dma((2, long)),
        ],
        compiler_params=pltpu.CompilerParams(
            collective_id=1, has_side_effects=True, vmem_limit_bytes=56 * 2**20
        ),
        cost_estimate=pl.CostEstimate(
            flops=10**7, bytes_accessed=2 * 10**7, transcendentals=0
        ),
    )(partials.reshape(block), stream)


def on_device(
    residual,
    prefill_qkv,
    decode_qkv,
    cache_pool,
    page_table,
    cache_len,
    out_weight,
    norm_gain,
    shared_gate_up,
    shared_down,
    shared_gate,
    routes,
    route_weight,
    expert_gate_up,
    expert_down,
):
    attended = attend(prefill_qkv, decode_qkv, cache_pool, page_table, cache_len)
    groups = lax.axis_size("exp")
    columns = lax.axis_size("req")
    tok_rows = residual.shape[0]
    model_width = out_weight.shape[1]
    line = (LINE, groups // LINE)
    rank_of, weight_of = dispatch_plan(routes, route_weight)
    rows = row_limit(routes.shape, groups)
    select = (
        (jnp.arange(rows, dtype=jnp.int32)[None, None, :, None] == rank_of[:, :, None, :])
        .astype(jnp.bfloat16)
        .reshape(line + (columns * rows, tok_rows))
    )
    stream, gathered, arrived = front(
        attended, out_weight, residual, norm_gain, select, line, columns
    )
    block_rows = gathered.reshape(groups * tok_rows, model_width)
    arrived = arrived.reshape(columns * groups * rows, model_width)

    gate_part = jnp.dot(block_rows, shared_gate_up[0], preferred_element_type=jnp.float32)
    up_part = jnp.dot(block_rows, shared_gate_up[1], preferred_element_type=jnp.float32)
    hidden = (jax.nn.silu(gate_part) * up_part).astype(jnp.bfloat16)
    shared_scale = jax.nn.sigmoid(
        jnp.dot(block_rows, shared_gate, preferred_element_type=jnp.float32)
    )
    shared = jnp.dot(hidden, shared_down, preferred_element_type=jnp.float32)
    shared = shared_scale[:, None] * shared

    expert_gate = jnp.dot(arrived, expert_gate_up[0, 0], preferred_element_type=jnp.float32)
    expert_up = jnp.dot(arrived, expert_gate_up[0, 1], preferred_element_type=jnp.float32)
    hidden = (jax.nn.silu(expert_gate) * expert_up).astype(jnp.bfloat16)
    answer = jnp.dot(hidden, expert_down[0], preferred_element_type=jnp.float32).astype(
        jnp.bfloat16
    )
    returned = lax.all_to_all(answer, "req", split_axis=0, concat_axis=0, tiled=True)
    returned = returned.reshape(columns, groups, rows, model_width)
    spread = jnp.where(
        jnp.arange(rows, dtype=jnp.int32)[None, None, :, None] == rank_of[:, :, None, :],
        weight_of[:, :, None, :],
        0.0,
    ).astype(jnp.bfloat16)
    routed = jnp.einsum("gcrt,cgrd->gtd", spread, returned, preferred_element_type=jnp.float32)
    partials = (shared.reshape(routed.shape) + routed).astype(jnp.bfloat16)
    return back(partials, stream, line)


def row_limit(routes_shape, groups):
    tok_rows, route_count = routes_shape
    return max(2, tok_rows * route_count * 2 // (EXP_COL * groups))


def dispatch_plan(routes, route_weight):
    groups = lax.axis_size("exp")
    columns = lax.axis_size("req")
    halves = columns // EXP_COL
    all_routes = lax.all_gather(routes.T, "exp", axis=0)
    all_weights = lax.all_gather(route_weight.T, "exp", axis=0)
    mine = (jnp.arange(columns, dtype=jnp.int32) * groups + lax.axis_index("exp")) // halves
    onehot = all_routes[:, None] == mine[None, :, None, None]
    named = jnp.any(onehot, axis=2).astype(jnp.int32)
    rank_of = jnp.where(named > 0, jnp.cumsum(named, axis=2) - 1, -1)
    weight_of = jnp.sum(jnp.where(onehot, all_weights[:, None], 0.0), axis=2)
    return rank_of, weight_of


def solution(mesh):
    placed = (
        P(("req", "exp"), None),
        P("req", None, None, "exp"),
        P("req", None, "exp"),
        P(None, "req", None, "exp"),
        P("req", None),
        P("req"),
        P("exp", None),
        P(),
        P(None, None, "exp"),
        P("exp", None),
        P(),
        P(("req", "exp"), None),
        P(("req", "exp"), None),
        P(("req", "exp"), None, None, None),
        P(("req", "exp"), None, None),
    )
    return jax.shard_map(
        on_device, mesh=mesh, in_specs=placed, out_specs=P(("req", "exp"), None), check_vma=False
    )
```

```python
import functools

import jax
import jax.numpy as jnp
from jax import lax
from jax.experimental import pallas as pl
from jax.experimental.pallas import tpu as pltpu
from jax.sharding import PartitionSpec as P

HD = 128
EXP_COL = 4
ROW_TILE = 16


NEG_FILL = -1e30
ROWS_BY_ROWS = (((1,), (1,)), ((), ()))


def attention_kernel(
    heads, q_ref, k_ref, v_ref, dq_ref, dk_ref, dv_ref, code_ref, ck_ref, cv_ref, out_ref,
    high_ref, sum_ref, acc_ref,
):
    step = pl.program_id(0)
    scaling = HD ** (-0.5)
    span_len = q_ref.shape[2]
    requests, width = dq_ref.shape
    rows = heads * requests

    query, keys, values = (q_ref[0, 0], k_ref[0, 0], v_ref[0, 0])
    half = span_len // 2
    base = pl.multiple_of((step // heads) * span_len, span_len)
    lane = pl.multiple_of((step % heads) * HD, HD)
    for lower, upper in ((0, half), (half, span_len)):
        scores = lax.dot_general(
            query[lower:upper], keys[:upper], ROWS_BY_ROWS, preferred_element_type=jnp.float32
        ) * scaling
        row = lax.broadcasted_iota(jnp.int32, scores.shape, 0) + lower
        column = lax.broadcasted_iota(jnp.int32, scores.shape, 1)
        scores = jnp.where(row >= column, scores, NEG_FILL)
        raised = jnp.exp(scores - jnp.max(scores, axis=-1, keepdims=True))
        total = jnp.sum(raised, axis=-1, keepdims=True)
        mixed = jnp.dot(
            raised.astype(jnp.bfloat16), values[:upper], preferred_element_type=jnp.float32
        )
        out_ref[pl.ds(base + lower, upper - lower), pl.ds(lane, HD)] = (mixed / total).astype(
            out_ref.dtype
        )

    head_of = lax.broadcasted_iota(jnp.int32, (rows, width), 0) // requests
    lane_head = lax.broadcasted_iota(jnp.int32, (rows, width), 1) // HD
    queries = jnp.where(
        head_of == lane_head,
        jnp.concatenate([dq_ref[...].astype(jnp.float32)] * heads, axis=0),
        0.0,
    )

    @pl.when(step == 0)
    def _():
        own = jnp.concatenate([dk_ref[...].astype(jnp.float32)] * heads, axis=0)
        high_ref[...] = jnp.sum(queries * own, axis=-1, keepdims=True) * scaling
        sum_ref[...] = jnp.ones_like(sum_ref)
        acc_ref[...] = jnp.concatenate([dv_ref[...].astype(jnp.float32)] * heads, axis=0)

    scores = lax.dot_general(
        queries.astype(jnp.bfloat16), ck_ref[0], ROWS_BY_ROWS, preferred_element_type=jnp.float32
    ) * scaling
    request = lax.broadcasted_iota(jnp.int32, scores.shape, 0) % requests
    allowed = request == code_ref[...]
    scores = jnp.where(allowed, scores, NEG_FILL)
    before = high_ref[...]
    after = jnp.maximum(before, jnp.max(scores, axis=-1, keepdims=True))
    raised = jnp.where(allowed, jnp.exp(scores - after), 0.0)
    fade = jnp.exp(before - after)
    high_ref[...] = after
    sum_ref[...] = sum_ref[...] * fade + jnp.sum(raised, axis=-1, keepdims=True)
    acc_ref[...] = acc_ref[...] * fade + jnp.dot(
        raised.astype(jnp.bfloat16), cv_ref[0], preferred_element_type=jnp.float32
    )

    @pl.when(step == pl.num_programs(0) - 1)
    def _():
        mixed = acc_ref[...] / sum_ref[...]
        first = out_ref.shape[0] - requests
        for head in range(heads):
            lanes = slice(head * HD, (head + 1) * HD)
            out_ref[first:, lanes] = mixed[
                head * requests : (head + 1) * requests, lanes
            ].astype(out_ref.dtype)


def attend(prefill_qkv, decode_qkv, cache_pool, page_table, cache_len):
    spans, _, span_len, width = prefill_qkv.shape
    requests = decode_qkv.shape[0]
    heads = width // HD
    steps = spans * heads
    pool_pages, page_len = (cache_pool.shape[1], cache_pool.shape[2])
    max_pages = page_table.shape[1]
    chunk = pool_pages // steps * page_len
    order = jnp.arange(max_pages, dtype=jnp.int32)
    left = cache_len[:, None] - order[None, :] * page_len
    held = (page_table[None] == jnp.arange(pool_pages, dtype=jnp.int32)[:, None, None]) & (
        left > 0
    )[None]
    owner = jnp.max(
        jnp.where(held, jnp.arange(requests, dtype=jnp.int32)[None, :, None], -1), axis=(1, 2)
    )
    valid = jnp.max(jnp.where(held, left[None], 0), axis=(1, 2))
    code = jnp.where(
        jnp.arange(page_len, dtype=jnp.int32)[None, :] < valid[:, None], owner[:, None], -1
    ).reshape(1, pool_pages * page_len)
    pool = cache_pool.reshape(2, pool_pages * page_len, width)
    whole = pl.BlockSpec((requests, width), lambda g: (0, 0))
    part = [
        pl.BlockSpec((1, 1, span_len, HD), functools.partial(lambda j, g: (g // heads, j, 0, g % heads), j))
        for j in range(3)
    ]
    out_rows = spans * span_len + requests
    return pl.pallas_call(
        functools.partial(attention_kernel, heads),
        grid=(steps,),
        in_specs=part
        + [whole] * 3
        + [
            pl.BlockSpec((1, chunk), lambda g: (0, g)),
            pl.BlockSpec((1, chunk, width), lambda g: (0, g, 0)),
            pl.BlockSpec((1, chunk, width), lambda g: (1, g, 0)),
        ],
        out_specs=pl.BlockSpec((out_rows, width), lambda g: (0, 0)),
        out_shape=jax.ShapeDtypeStruct((out_rows, width), jnp.bfloat16),
        scratch_shapes=[
            pltpu.VMEM((heads * requests, 1), jnp.float32),
            pltpu.VMEM((heads * requests, 1), jnp.float32),
            pltpu.VMEM((heads * requests, width), jnp.float32),
        ],
        compiler_params=pltpu.CompilerParams(vmem_limit_bytes=40 * 2**20),
        cost_estimate=pl.CostEstimate(
            flops=2 * 10**9, bytes_accessed=2 * pool.size + 2 * prefill_qkv.size, transcendentals=2 * 10**6
        ),
    )(
        prefill_qkv, prefill_qkv, prefill_qkv,
        decode_qkv[:, 0], decode_qkv[:, 1], decode_qkv[:, 2],
        code, pool, pool,
    )


LINE = 4
MESH = pl.DeviceIdType.MESH


def greet(place, line, groups, columns, all_groups):
    outer, inner = place
    long, short = line
    barrier = pltpu.get_barrier_semaphore()
    count = jnp.int32(0)
    if all_groups:
        exp = outer * short + inner
        for k in range(1, groups):
            pl.semaphore_signal(
                barrier, inc=1, device_id={"exp": (exp + k) % groups}, device_id_type=MESH
            )
        count = count + (groups - 1)
    for ok, target in () if all_groups else (
        (outer > 0, (outer - 1) * short + inner),
        (outer < long - 1, (outer + 1) * short + inner),
        (inner > 0, outer * short + inner - 1),
        (inner < short - 1, outer * short + inner + 1),
    ):
        @pl.when(ok)
        def _():
            pl.semaphore_signal(barrier, inc=1, device_id={"exp": target}, device_id_type=MESH)

        count = count + ok.astype(jnp.int32)
    if columns > 1:
        me = lax.axis_index("req")
        for k in range(1, columns):
            pl.semaphore_signal(
                barrier, inc=1, device_id={"req": (me + k) % columns}, device_id_type=MESH
            )
        count = count + (columns - 1)
    pl.semaphore_wait(barrier, count)


def visit(place, long, farthest_first, body):
    outer = place[0]
    distances = range(long - 1, -1, -1) if farthest_first else range(long)
    for distance in distances:
        @pl.when(outer + distance < long)
        def _():
            body(outer + distance, distance, 0)

        if distance > 0:
            @pl.when(outer - distance >= 0)
            def _():
                body(outer - distance, distance, 1)


def reduce_scatter(place, line, part, fill, column, rin, rout, total, sems):
    outer, inner = place
    long, short = line
    isend, irecv, osend, orecv = sems

    def inner_copy(way, o, i, relay):
        target = outer * short + inner + (1 if way == 0 else -1)
        return pltpu.make_async_remote_copy(
            src_ref=(rin.at[way, o, i] if relay else part.at[o, i]),
            dst_ref=rin.at[way, o, i],
            send_sem=isend.at[way, o, i],
            recv_sem=irecv.at[way, o, i],
            device_id={"exp": target},
            device_id_type=MESH,
        )

    def outer_copy(way, o):
        target = (outer + (1 if way == 0 else -1)) * short + inner
        return pltpu.make_async_remote_copy(
            src_ref=column.at[o],
            dst_ref=rout.at[way, o],
            send_sem=osend.at[way, o],
            recv_sem=orecv.at[way, o],
            device_id={"exp": target},
            device_id_type=MESH,
        )

    def first(o, distance, side):
        fill(o)
        for way in (0, 1):
            for gap in range(short - 1, 0, -1):
                i = inner + gap if way == 0 else inner - gap
                ok = (i < short) if way == 0 else (i >= 0)
                behind = (inner > 0) if way == 0 else (inner < short - 1)
                if short == 2:
                    @pl.when(ok)
                    def _():
                        inner_copy(way, o, i, False).start()
                else:
                    @pl.when(ok & jnp.logical_not(behind))
                    def _():
                        inner_copy(way, o, i, False).start()

    visit(place, long, True, first)

    def second(o, distance, side):
        if short > 2:
            for way in (0, 1):
                for gap in range(short - 1, 0, -1):
                    i = inner + gap if way == 0 else inner - gap
                    ok = (i < short) if way == 0 else (i >= 0)
                    behind = (inner > 0) if way == 0 else (inner < short - 1)

                    @pl.when(ok & behind)
                    def _():
                        inner_copy(way, o, i, True).wait_recv()
                        rin[way, o, i] = (
                            rin[way, o, i].astype(jnp.float32) + part[o, i].astype(jnp.float32)
                        ).astype(jnp.bfloat16)
                        inner_copy(way, o, i, True).start()

        total[...] = part[o, inner].astype(jnp.float32)
        for way, behind in ((0, inner > 0), (1, inner < short - 1)):
            @pl.when(behind)
            def _():
                inner_copy(way, o, inner, False).wait_recv()
                total[...] += rin[way, o, inner].astype(jnp.float32)

        for way, behind in ((0, outer > 0), (1, outer < long - 1)):
            if distance == 0 or way == side:
                @pl.when(behind)
                def _():
                    outer_copy(way, o).wait_recv()
                    total[...] += rout[way, o].astype(jnp.float32)

        if distance > 0:
            column[o] = total[...].astype(jnp.bfloat16)
            outer_copy(side, o).start()

    visit(place, long, True, second)

    def finish():
        for o in range(long):
            for i in range(short):
                @pl.when(inner < i)
                def _():
                    inner_copy(0, o, i, False).wait_send()

                @pl.when(inner > i)
                def _():
                    inner_copy(1, o, i, False).wait_send()

            @pl.when(outer < o)
            def _():
                outer_copy(0, o).wait_send()

            @pl.when(outer > o)
            def _():
                outer_copy(1, o).wait_send()

    return finish


def slots_of(plan, exp, columns, groups, rows):
    tokens = plan.shape[1]
    routes = plan[: plan.shape[0] // 2]
    halves = columns // EXP_COL
    hits = [
        routes == ((c * groups + exp) // halves).astype(jnp.float32) for c in range(columns)
    ]
    named = jnp.concatenate(
        [jnp.max(hit.astype(jnp.float32), axis=0, keepdims=True) for hit in hits], axis=0
    )
    upto = lax.broadcasted_iota(jnp.int32, (tokens, tokens), 0) <= lax.broadcasted_iota(
        jnp.int32, (tokens, tokens), 1
    )
    rank = jnp.dot(
        named.astype(jnp.bfloat16), upto.astype(jnp.bfloat16), preferred_element_type=jnp.float32
    )
    rank = jnp.where(named > 0.0, rank - 1.0, -1.0).astype(jnp.int32)
    slot = lax.broadcasted_iota(jnp.int32, (rows, tokens), 0)
    return hits, [slot == rank[c : c + 1] for c in range(columns)]


def front_kernel(
    line, columns, att_ref, w_ref, res_ref, gain_ref, mine_ref, stream_ref, all_ref, arr_ref,
    plan_ref, part, column, rin, rout, total, pack, isend, irecv, osend, orecv, asend, arecv, ysend, yrecv,
    psend, precv,
):
    long, short = line
    groups = long * short
    exp = lax.axis_index("exp")
    me = lax.axis_index("req")
    place = (exp // short, exp % short)
    outer, inner = place
    greet(place, line, groups, columns, True)

    def plan_copy(k):
        return pltpu.make_async_remote_copy(
            src_ref=mine_ref,
            dst_ref=plan_ref.at[outer, inner],
            send_sem=psend.at[k],
            recv_sem=precv.at[k],
            device_id={"exp": (exp + k) % groups},
            device_id_type=MESH,
        )

    for k in range(1, groups):
        plan_copy(k).start()
    plan_ref[outer, inner] = mine_ref[...]

    def fill(o):
        for i in range(short):
            part[o, i] = jnp.dot(
                att_ref[o, i], w_ref[...], preferred_element_type=jnp.float32
            ).astype(jnp.bfloat16)

    finish = reduce_scatter(
        place, line, part, fill, column, rin, rout, total, (isend, irecv, osend, orecv)
    )
    for k in range(1, groups):
        plan_copy(k).wait_recv()
    stream = (res_ref[...].astype(jnp.float32) + total[...]).astype(jnp.bfloat16)
    stream_ref[...] = stream
    wide = stream.astype(jnp.float32)
    all_ref[outer, inner] = (
        wide
        * lax.rsqrt(jnp.mean(wide * wide, axis=-1, keepdims=True) + 1e-06)
        * gain_ref[...]
    ).astype(jnp.bfloat16)

    def pass_on(way, o, i):
        target = exp + (short, -short, 1, -1)[way]
        return pltpu.make_async_remote_copy(
            src_ref=all_ref.at[o, i],
            dst_ref=all_ref.at[o, i],
            send_sem=asend.at[way, o, i],
            recv_sem=arecv.at[o, i],
            device_id={"exp": target},
            device_id_type=MESH,
        )

    def to_column(k, o, i):
        target = (me + k) % columns
        return pltpu.make_async_remote_copy(
            src_ref=pack.at[o, i, target],
            dst_ref=arr_ref.at[o, me, i],
            send_sem=ysend.at[k, o, i],
            recv_sem=yrecv.at[k, o, i],
            device_id={"req": target},
            device_id_type=MESH,
        )

    def dispatch(o, i):
        taken = slots_of(plan_ref[o, i], exp, columns, groups, pack.shape[3])[1]
        select = jnp.concatenate([each.astype(jnp.float32) for each in taken], axis=0)
        rows = jnp.dot(
            select.astype(jnp.bfloat16), all_ref[o, i], preferred_element_type=jnp.float32
        ).astype(jnp.bfloat16)
        pack[o, i] = rows.reshape(pack.shape[2:])
        for k in range(1, columns):
            to_column(k, o, i).start()
        arr_ref[o, me, i] = pack[o, i, me]

    def spread(o, distance, side):
        if distance > 0:
            pass_on(0, o, inner).wait_recv()
        for way, ahead in ((0, outer < long - 1), (1, outer > 0)):
            if distance == 0 or way == 1 - side:
                @pl.when(ahead)
                def _():
                    pass_on(way, o, inner).start()
        for way, ahead in ((2, inner < short - 1), (3, inner > 0)):
            @pl.when(ahead)
            def _():
                pass_on(way, o, inner).start()
        dispatch(o, inner)

    def across(o, distance, side):
        for gap in range(1, short):
            for way, i, ok, ahead in (
                (2, inner - gap, inner - gap >= 0, inner < short - 1),
                (3, inner + gap, inner + gap < short, inner > 0),
            ):
                @pl.when(ok)
                def _():
                    pass_on(way, o, i).wait_recv()
                    if short > 2:
                        @pl.when(ahead)
                        def _():
                            pass_on(way, o, i).start()
                    dispatch(o, i)

    for step in range(long + 1):
        if step < long:
            near(place, long, step, spread)
        if step > 0:
            near(place, long, step - 1, across)

    finish()
    for k in range(1, groups):
        plan_copy(k).wait_send()
    for o in range(long):
        for i in range(short):
            at_line = inner == i
            @pl.when(at_line & (outer >= o) & (outer < long - 1))
            def _():
                pass_on(0, o, i).wait_send()

            @pl.when(at_line & (outer <= o) & (outer > 0))
            def _():
                pass_on(1, o, i).wait_send()

            @pl.when((inner >= i) & (inner < short - 1))
            def _():
                pass_on(2, o, i).wait_send()

            @pl.when((inner <= i) & (inner > 0))
            def _():
                pass_on(3, o, i).wait_send()

            for k in range(1, columns):
                to_column(k, o, i).wait_send()
                to_column(k, o, i).wait_recv()


def near(place, long, distance, body):
    outer = place[0]

    @pl.when(outer + distance < long)
    def _():
        body(outer + distance, distance, 0)

    if distance > 0:
        @pl.when(outer - distance >= 0)
        def _():
            body(outer - distance, distance, 1)


def front(attended, out_weight, residual, norm_gain, plan, rows, line, columns):
    long, short = line
    tokens, width = residual.shape
    depth = out_weight.shape[0]
    dma = pltpu.SemaphoreType.DMA
    block = (long, short, tokens, width)
    vmem = pl.BlockSpec(memory_space=pltpu.VMEM)
    bf16 = jnp.bfloat16
    return pl.pallas_call(
        functools.partial(front_kernel, line, columns),
        out_shape=(
            jax.ShapeDtypeStruct((tokens, width), bf16),
            jax.ShapeDtypeStruct(block, bf16),
            jax.ShapeDtypeStruct((long, columns, short, rows, width), bf16),
            jax.ShapeDtypeStruct((long, short) + plan.shape, jnp.float32),
        ),
        in_specs=[vmem] * 5,
        out_specs=(vmem, vmem, vmem, vmem),
        scratch_shapes=[
            pltpu.VMEM(block, bf16),
            pltpu.VMEM((long, tokens, width), bf16),
            pltpu.VMEM((2,) + block, bf16),
            pltpu.VMEM((2, long, tokens, width), bf16),
            pltpu.VMEM((tokens, width), jnp.float32),
            pltpu.VMEM((long, short, columns, rows, width), bf16),
            dma((2, long, short)),
            dma((2, long, short)),
            dma((2, long)),
            dma((2, long)),
            dma((4, long, short)),
            dma((long, short)),
            dma((columns, long, short)),
            dma((columns, long, short)),
            dma((long * short,)),
            dma((long * short,)),
        ],
        compiler_params=pltpu.CompilerParams(
            collective_id=0, has_side_effects=True, vmem_limit_bytes=56 * 2**20
        ),
        cost_estimate=pl.CostEstimate(
            flops=4 * 10**9, bytes_accessed=2 * 10**7, transcendentals=0
        ),
    )(
        attended.reshape(long, short, tokens, depth), out_weight, residual,
        norm_gain.reshape(1, width), plan,
    )


def order_of(k, place, long):
    outer = place[0]
    low = jnp.where(2 * outer <= long - 1, outer, long - 1 - outer)
    skip = long - 1 - 2 * low
    pair = jnp.maximum(k - skip, 0)
    gap = low - pair // 2
    o = jnp.where(k < skip, long - 1 - k, low + gap * (1 - 2 * (pair % 2)))
    return jnp.where(2 * outer <= long - 1, o, long - 1 - o)


def tiles(width, step):
    return [(lower, min(lower + step, width)) for lower in range(0, width, step)]


def back_kernel(
    line, columns, arr_ref, all_ref, eg_ref, ed_ref, sg_ref, sd_ref, gate_ref, plan_ref,
    stream_ref, out_ref, rows, part, eg, ed, sg, sd, ret, rin, rout, column, total, hidden,
    shidden, load, isend, irecv, osend, orecv, ysend, yrecv,
):
    long, short = line
    exp = lax.axis_index("exp")
    me = lax.axis_index("req")
    place = (exp // short, exp % short)
    outer, inner = place
    width = eg.shape[1]
    bf16, f32 = (jnp.bfloat16, jnp.float32)

    load_rows = pltpu.make_async_copy(arr_ref, rows, load.at[0])
    load_eg = pltpu.make_async_copy(eg_ref.at[0], eg, load.at[1])
    load_ed = pltpu.make_async_copy(ed_ref.at[0], ed, load.at[2])
    load_sg = pltpu.make_async_copy(sg_ref, sg, load.at[3])
    load_sd = pltpu.make_async_copy(sd_ref, sd, load.at[4])
    load_all = pltpu.make_async_copy(all_ref, part, load.at[5])
    for copy in (load_rows, load_eg, load_ed, load_sg, load_sd, load_all):
        copy.start()
    greet(place, line, long * short, columns, False)

    def answer_copy(k, o):
        target = (me + k) % columns
        return pltpu.make_async_remote_copy(
            src_ref=rows.at[o, target],
            dst_ref=ret.at[o, me],
            send_sem=ysend.at[k, o],
            recv_sem=yrecv.at[k, o],
            device_id={"req": target},
            device_id_type=MESH,
        )

    load_rows.wait()
    load_eg.wait()
    load_ed.wait()

    def expert(k, carry):
        o = order_of(k, place, long)
        x = rows[o].reshape(hidden.shape[0], width)
        for lower, upper in tiles(eg.shape[2], 256):
            gate = jnp.dot(x, eg[0, :, lower:upper], preferred_element_type=f32)
            up = jnp.dot(x, eg[1, :, lower:upper], preferred_element_type=f32)
            hidden[:, lower:upper] = (jax.nn.silu(gate) * up).astype(bf16)
        for lower, upper in tiles(width, 512):
            down = jnp.dot(hidden[...], ed[:, lower:upper], preferred_element_type=f32)
            rows[o, :, :, :, lower:upper] = down.astype(bf16).reshape(
                rows.shape[1:4] + (upper - lower,)
            )
        for j in range(1, columns):
            answer_copy(j, o).start()
        ret[o, me] = rows[o, me]
        return carry

    lax.fori_loop(0, long, expert, 0)
    load_sg.wait()
    load_sd.wait()
    load_all.wait()

    def inner_copy(way, o, i, relay):
        slot = rin.at[o, i + 1 - way]
        return pltpu.make_async_remote_copy(
            src_ref=(slot if relay else part.at[o, i]),
            dst_ref=slot,
            send_sem=isend.at[way, o, i],
            recv_sem=irecv.at[way, o, i],
            device_id={"exp": outer * short + inner + 1 - 2 * way},
            device_id_type=MESH,
        )

    def outer_copy(way, o):
        return pltpu.make_async_remote_copy(
            src_ref=column.at[o],
            dst_ref=rout.at[o + 1 - way],
            send_sem=osend.at[way, o],
            recv_sem=orecv.at[way, o],
            device_id={"exp": (outer + 1 - 2 * way) * short + inner},
            device_id_type=MESH,
        )

    def toward(way, gap):
        i = inner + gap * (1 - 2 * way)
        ok = (i < short) if way == 0 else (i >= 0)
        behind = (inner > 0) if way == 0 else (inner < short - 1)
        return i, ok, behind

    def fill(o):
        for i in range(short):
            x = part[o, i]
            scale = jax.nn.sigmoid(
                jnp.sum(x.astype(f32) * gate_ref[...].astype(f32), axis=-1, keepdims=True)
            )
            for lower, upper in tiles(sg.shape[1], 256):
                gate = lax.dot_general(
                    x, sg[0, lower:upper], ROWS_BY_ROWS, preferred_element_type=f32
                )
                up = lax.dot_general(
                    x, sg[1, lower:upper], ROWS_BY_ROWS, preferred_element_type=f32
                )
                shidden[:, lower:upper] = (jax.nn.silu(gate) * up).astype(bf16)
            for lower, upper in tiles(width, 512):
                down = jnp.dot(shidden[...], sd[:, lower:upper], preferred_element_type=f32)
                part[o, i, :, lower:upper] = (scale * down).astype(bf16)
        for j in range(1, columns):
            answer_copy(j, o).wait_recv()
        for i in range(short):
            hits, taken = slots_of(
                plan_ref[o, i], exp, columns, long * short, rows.shape[3]
            )
            weights = plan_ref[o, i, plan_ref.shape[2] // 2 :]
            spread = jnp.concatenate(
                [
                    jnp.where(
                        taken[c],
                        jnp.sum(
                            jnp.where(hits[c], weights, 0.0), axis=0, keepdims=True
                        ),
                        0.0,
                    )
                    for c in range(columns)
                ],
                axis=0,
            ).astype(bf16)
            for lower, upper in tiles(width, 512):
                picked = ret[o, :, i, :, lower:upper].reshape(-1, upper - lower)
                routed = lax.dot_general(
                    spread, picked, (((0,), (0,)), ((), ())), preferred_element_type=f32
                )
                part[o, i, :, lower:upper] = (
                    part[o, i, :, lower:upper].astype(f32) + routed
                ).astype(bf16)

    def first(o):
        fill(o)
        for way in (0, 1):
            for gap in range(short - 1, 0, -1):
                i, ok, behind = toward(way, gap)
                if short > 2:
                    ok = ok & jnp.logical_not(behind)

                @pl.when(ok)
                def _():
                    inner_copy(way, o, i, False).start()

    def second(o, own):
        if short > 2:
            for way in (0, 1):
                for gap in range(short - 1, 0, -1):
                    i, ok, behind = toward(way, gap)

                    @pl.when(ok & behind)
                    def _():
                        inner_copy(way, o, i, True).wait_recv()
                        slot = i + 1 - way
                        rin[o, slot] = (
                            rin[o, slot].astype(f32) + part[o, i].astype(f32)
                        ).astype(bf16)
                        inner_copy(way, o, i, True).start()

        total[...] = part[o, inner].astype(f32)
        for way, behind in ((0, inner > 0), (1, inner < short - 1)):
            @pl.when(behind)
            def _():
                inner_copy(way, o, inner, False).wait_recv()
                total[...] += rin[o, inner + 1 - way].astype(f32)

        for way, behind in ((0, outer > 0), (1, outer < long - 1)):
            if not own:
                behind = behind & ((o > outer) if way == 0 else (o < outer))

            @pl.when(behind)
            def _():
                outer_copy(way, o).wait_recv()
                total[...] += rout[o + 1 - way].astype(f32)

        if not own:
            column[o] = total[...].astype(bf16)
            for way, ahead in ((0, o > outer), (1, o < outer)):
                @pl.when(ahead)
                def _():
                    outer_copy(way, o).start()

    def combine(k, carry):
        first(order_of(k, place, long))

        @pl.when(k > 0)
        def _():
            second(order_of(k - 1, place, long), False)

        return carry

    lax.fori_loop(0, long, combine, 0)
    second(outer, True)
    out_ref[...] = (stream_ref[...].astype(f32) + total[...]).astype(bf16)

    for o in range(long):
        for i in range(short):
            @pl.when(inner < i)
            def _():
                inner_copy(0, o, i, False).wait_send()

            @pl.when(inner > i)
            def _():
                inner_copy(1, o, i, False).wait_send()

        @pl.when(outer < o)
        def _():
            outer_copy(0, o).wait_send()

        @pl.when(outer > o)
        def _():
            outer_copy(1, o).wait_send()

        for j in range(1, columns):
            answer_copy(j, o).wait_send()


def back(
    arrived, gathered, expert_gate_up, expert_down, shared_gate_up, shared_down, shared_gate,
    plan, stream, line, columns,
):
    long, short = line
    tokens, width = stream.shape
    count = arrived.shape[3]
    hid, shid = (expert_down.shape[1], shared_down.shape[0])
    dma = pltpu.SemaphoreType.DMA
    block = (long, short, tokens, width)
    vmem = pl.BlockSpec(memory_space=pltpu.VMEM)
    hbm = pl.BlockSpec(memory_space=pl.ANY)
    bf16 = jnp.bfloat16
    return pl.pallas_call(
        functools.partial(back_kernel, line, columns),
        out_shape=jax.ShapeDtypeStruct((tokens, width), bf16),
        in_specs=[hbm] * 6 + [vmem] * 3,
        out_specs=vmem,
        scratch_shapes=[
            pltpu.VMEM(arrived.shape, bf16),
            pltpu.VMEM(block, bf16),
            pltpu.VMEM(expert_gate_up.shape[1:], bf16),
            pltpu.VMEM(expert_down.shape[1:], bf16),
            pltpu.VMEM(shared_gate_up.shape, bf16),
            pltpu.VMEM(shared_down.shape, bf16),
            pltpu.VMEM(arrived.shape, bf16),
            pltpu.VMEM((long, short + 1, tokens, width), bf16),
            pltpu.VMEM((long + 1, tokens, width), bf16),
            pltpu.VMEM((long, tokens, width), bf16),
            pltpu.VMEM((tokens, width), jnp.float32),
            pltpu.VMEM((columns * short * count, hid), bf16),
            pltpu.VMEM((tokens, shid), bf16),
            dma((6,)),
            dma((2, long, short)),
            dma((2, long, short)),
            dma((2, long)),
            dma((2, long)),
            dma((columns, long)),
            dma((columns, long)),
        ],
        compiler_params=pltpu.CompilerParams(
            collective_id=1, has_side_effects=True, vmem_limit_bytes=60 * 2**20
        ),
        cost_estimate=pl.CostEstimate(
            flops=3 * 10**10, bytes_accessed=5 * 10**7, transcendentals=0
        ),
    )(
        arrived, gathered, expert_gate_up, expert_down, shared_gate_up, shared_down,
        shared_gate.reshape(1, width), plan, stream,
    )


def on_device(
    residual,
    prefill_qkv,
    decode_qkv,
    cache_pool,
    page_table,
    cache_len,
    out_weight,
    norm_gain,
    shared_gate_up,
    shared_down,
    shared_gate,
    routes,
    route_weight,
    expert_gate_up,
    expert_down,
):
    attended = attend(prefill_qkv, decode_qkv, cache_pool, page_table, cache_len)
    groups = lax.axis_size("exp")
    columns = lax.axis_size("req")
    line = (LINE, groups // LINE)
    plan = jnp.concatenate([routes.T.astype(jnp.float32), route_weight.T], axis=0)
    rows = row_limit(routes.shape, groups)
    stream, gathered, arrived, plan = front(
        attended, out_weight, residual, norm_gain, plan, rows, line, columns
    )
    return back(
        arrived, gathered, expert_gate_up, expert_down, jnp.swapaxes(shared_gate_up, 1, 2),
        shared_down, shared_gate, plan, stream, line, columns,
    )


def row_limit(routes_shape, groups):
    tok_rows, route_count = routes_shape
    return max(2, tok_rows * route_count * 2 // (EXP_COL * groups))


def solution(mesh):
    placed = (
        P(("req", "exp"), None),
        P("req", None, None, "exp"),
        P("req", None, "exp"),
        P(None, "req", None, "exp"),
        P("req", None),
        P("req"),
        P("exp", None),
        P(),
        P(None, None, "exp"),
        P("exp", None),
        P(),
        P(("req", "exp"), None),
        P(("req", "exp"), None),
        P(("req", "exp"), None, None, None),
        P(("req", "exp"), None, None),
    )
    return jax.shard_map(
        on_device, mesh=mesh, in_specs=placed, out_specs=P(("req", "exp"), None), check_vma=False
    )
```

```python
import functools

import jax
import jax.numpy as jnp
from jax import lax
from jax.experimental import pallas as pl
from jax.experimental.pallas import tpu as pltpu
from jax.sharding import PartitionSpec as P

HD = 128
EXP_COL = 4
ROW_TILE = 16


NEG_FILL = -1e30
ROWS_BY_ROWS = (((1,), (1,)), ((), ()))


def attention_kernel(
    heads, q_ref, k_ref, v_ref, dq_ref, dk_ref, dv_ref, code_ref, ck_ref, cv_ref, out_ref,
    high_ref, sum_ref, acc_ref,
):
    step = pl.program_id(0)
    scaling = HD ** (-0.5)
    span_len = q_ref.shape[2]
    requests, width = dq_ref.shape
    rows = heads * requests

    query, keys, values = (q_ref[0, 0], k_ref[0, 0], v_ref[0, 0])
    half = span_len // 2
    base = pl.multiple_of((step // heads) * span_len, span_len)
    lane = pl.multiple_of((step % heads) * HD, HD)
    for lower, upper in ((0, half), (half, span_len)):
        scores = lax.dot_general(
            query[lower:upper], keys[:upper], ROWS_BY_ROWS, preferred_element_type=jnp.float32
        ) * scaling
        row = lax.broadcasted_iota(jnp.int32, scores.shape, 0) + lower
        column = lax.broadcasted_iota(jnp.int32, scores.shape, 1)
        scores = jnp.where(row >= column, scores, NEG_FILL)
        raised = jnp.exp(scores - jnp.max(scores, axis=-1, keepdims=True))
        total = jnp.sum(raised, axis=-1, keepdims=True)
        mixed = jnp.dot(
            raised.astype(jnp.bfloat16), values[:upper], preferred_element_type=jnp.float32
        )
        out_ref[pl.ds(base + lower, upper - lower), pl.ds(lane, HD)] = (mixed / total).astype(
            out_ref.dtype
        )

    head_of = lax.broadcasted_iota(jnp.int32, (rows, width), 0) // requests
    lane_head = lax.broadcasted_iota(jnp.int32, (rows, width), 1) // HD
    queries = jnp.where(
        head_of == lane_head,
        jnp.concatenate([dq_ref[...].astype(jnp.float32)] * heads, axis=0),
        0.0,
    )

    @pl.when(step == 0)
    def _():
        own = jnp.concatenate([dk_ref[...].astype(jnp.float32)] * heads, axis=0)
        high_ref[...] = jnp.sum(queries * own, axis=-1, keepdims=True) * scaling
        sum_ref[...] = jnp.ones_like(sum_ref)
        acc_ref[...] = jnp.concatenate([dv_ref[...].astype(jnp.float32)] * heads, axis=0)

    scores = lax.dot_general(
        queries.astype(jnp.bfloat16), ck_ref[0], ROWS_BY_ROWS, preferred_element_type=jnp.float32
    ) * scaling
    request = lax.broadcasted_iota(jnp.int32, scores.shape, 0) % requests
    allowed = request == code_ref[...]
    scores = jnp.where(allowed, scores, NEG_FILL)
    before = high_ref[...]
    after = jnp.maximum(before, jnp.max(scores, axis=-1, keepdims=True))
    raised = jnp.where(allowed, jnp.exp(scores - after), 0.0)
    fade = jnp.exp(before - after)
    high_ref[...] = after
    sum_ref[...] = sum_ref[...] * fade + jnp.sum(raised, axis=-1, keepdims=True)
    acc_ref[...] = acc_ref[...] * fade + jnp.dot(
        raised.astype(jnp.bfloat16), cv_ref[0], preferred_element_type=jnp.float32
    )

    @pl.when(step == pl.num_programs(0) - 1)
    def _():
        mixed = acc_ref[...] / sum_ref[...]
        first = out_ref.shape[0] - requests
        for head in range(heads):
            lanes = slice(head * HD, (head + 1) * HD)
            out_ref[first:, lanes] = mixed[
                head * requests : (head + 1) * requests, lanes
            ].astype(out_ref.dtype)


def attend(prefill_qkv, decode_qkv, cache_pool, page_table, cache_len):
    spans, _, span_len, width = prefill_qkv.shape
    requests = decode_qkv.shape[0]
    heads = width // HD
    steps = spans * heads
    pool_pages, page_len = (cache_pool.shape[1], cache_pool.shape[2])
    max_pages = page_table.shape[1]
    chunk = pool_pages // steps * page_len
    order = jnp.arange(max_pages, dtype=jnp.int32)
    left = cache_len[:, None] - order[None, :] * page_len
    held = (page_table[None] == jnp.arange(pool_pages, dtype=jnp.int32)[:, None, None]) & (
        left > 0
    )[None]
    owner = jnp.max(
        jnp.where(held, jnp.arange(requests, dtype=jnp.int32)[None, :, None], -1), axis=(1, 2)
    )
    valid = jnp.max(jnp.where(held, left[None], 0), axis=(1, 2))
    code = jnp.where(
        jnp.arange(page_len, dtype=jnp.int32)[None, :] < valid[:, None], owner[:, None], -1
    ).reshape(1, pool_pages * page_len)
    pool = cache_pool.reshape(2, pool_pages * page_len, width)
    whole = pl.BlockSpec((requests, width), lambda g: (0, 0))
    part = [
        pl.BlockSpec((1, 1, span_len, HD), functools.partial(lambda j, g: (g // heads, j, 0, g % heads), j))
        for j in range(3)
    ]
    out_rows = spans * span_len + requests
    return pl.pallas_call(
        functools.partial(attention_kernel, heads),
        grid=(steps,),
        in_specs=part
        + [whole] * 3
        + [
            pl.BlockSpec((1, chunk), lambda g: (0, g)),
            pl.BlockSpec((1, chunk, width), lambda g: (0, g, 0)),
            pl.BlockSpec((1, chunk, width), lambda g: (1, g, 0)),
        ],
        out_specs=pl.BlockSpec((out_rows, width), lambda g: (0, 0)),
        out_shape=jax.ShapeDtypeStruct((out_rows, width), jnp.bfloat16),
        scratch_shapes=[
            pltpu.VMEM((heads * requests, 1), jnp.float32),
            pltpu.VMEM((heads * requests, 1), jnp.float32),
            pltpu.VMEM((heads * requests, width), jnp.float32),
        ],
        compiler_params=pltpu.CompilerParams(vmem_limit_bytes=40 * 2**20),
        cost_estimate=pl.CostEstimate(
            flops=2 * 10**9, bytes_accessed=2 * pool.size + 2 * prefill_qkv.size, transcendentals=2 * 10**6
        ),
    )(
        prefill_qkv, prefill_qkv, prefill_qkv,
        decode_qkv[:, 0], decode_qkv[:, 1], decode_qkv[:, 2],
        code, pool, pool,
    )


LINE = 4
MESH = pl.DeviceIdType.MESH


def greet(place, line, groups, columns, all_groups):
    outer, inner = place
    long, short = line
    barrier = pltpu.get_barrier_semaphore()
    count = jnp.int32(0)
    if all_groups:
        exp = outer * short + inner
        for k in range(1, groups):
            pl.semaphore_signal(
                barrier, inc=1, device_id={"exp": (exp + k) % groups}, device_id_type=MESH
            )
        count = count + (groups - 1)
    for ok, target in () if all_groups else (
        (outer > 0, (outer - 1) * short + inner),
        (outer < long - 1, (outer + 1) * short + inner),
        (inner > 0, outer * short + inner - 1),
        (inner < short - 1, outer * short + inner + 1),
    ):
        @pl.when(ok)
        def _():
            pl.semaphore_signal(barrier, inc=1, device_id={"exp": target}, device_id_type=MESH)

        count = count + ok.astype(jnp.int32)
    if columns > 1:
        me = lax.axis_index("req")
        for k in range(1, columns):
            pl.semaphore_signal(
                barrier, inc=1, device_id={"req": (me + k) % columns}, device_id_type=MESH
            )
        count = count + (columns - 1)
    pl.semaphore_wait(barrier, count)


def slots_of(plan, exp, columns, groups, rows):
    tokens = plan.shape[1]
    routes = plan[: plan.shape[0] // 2]
    halves = columns // EXP_COL
    hits = [
        routes == ((c * groups + exp) // halves).astype(jnp.float32) for c in range(columns)
    ]
    named = jnp.concatenate(
        [jnp.max(hit.astype(jnp.float32), axis=0, keepdims=True) for hit in hits], axis=0
    )
    upto = lax.broadcasted_iota(jnp.int32, (tokens, tokens), 0) <= lax.broadcasted_iota(
        jnp.int32, (tokens, tokens), 1
    )
    rank = jnp.dot(
        named.astype(jnp.bfloat16), upto.astype(jnp.bfloat16), preferred_element_type=jnp.float32
    )
    rank = jnp.where(named > 0.0, rank - 1.0, -1.0).astype(jnp.int32)
    slot = lax.broadcasted_iota(jnp.int32, (rows, tokens), 0)
    return hits, [slot == rank[c : c + 1] for c in range(columns)]


def front_kernel(
    line, columns, att_ref, w_refs, res_ref, gain_ref, mine_ref, stream_ref, all_ref, arr_ref,
    plan_ref, attin, column, rout, total, pack, isend, irecv, osend, orecv, asend, arecv, bsend,
    brecv, ysend, yrecv, psend, precv,
):
    long, short = line
    groups = long * short
    exp = lax.axis_index("exp")
    me = lax.axis_index("req")
    place = (exp // short, exp % short)
    outer, inner = place
    f32, bf16 = (jnp.float32, jnp.bfloat16)
    direct = all_ref.shape[3] // 8 // 128 * 128 if short == 2 else 0
    greet(place, line, groups, columns, True)

    def rows_copy(k, o):
        target = (inner + k) % short
        return pltpu.make_async_remote_copy(
            src_ref=att_ref.at[o, target],
            dst_ref=attin.at[k, o],
            send_sem=isend.at[k, o],
            recv_sem=irecv.at[k, o],
            device_id={"exp": outer * short + target},
            device_id_type=MESH,
        )

    def outer_copy(way, o):
        return pltpu.make_async_remote_copy(
            src_ref=column.at[o],
            dst_ref=rout.at[o + 1 - way],
            send_sem=osend.at[way, o],
            recv_sem=orecv.at[way, o],
            device_id={"exp": (outer + 1 - 2 * way) * short + inner},
            device_id_type=MESH,
        )

    def plan_copy(k):
        return pltpu.make_async_remote_copy(
            src_ref=mine_ref,
            dst_ref=plan_ref.at[outer, inner],
            send_sem=psend.at[k],
            recv_sem=precv.at[k],
            device_id={"exp": (exp + k) % groups},
            device_id_type=MESH,
        )

    def send_rows(n, carry):
        for k in range(1, short):
            rows_copy(k, order_of(n, place, long)).start()
        return carry

    lax.fori_loop(0, long, send_rows, 0)
    for k in range(1, groups):
        plan_copy(k).start()
    plan_ref[outer, inner] = mine_ref[...]

    def project(o, own):
        total[...] = jnp.dot(att_ref[o, inner], w_refs[0][...], preferred_element_type=f32)
        for k in range(1, short):
            rows_copy(k, o).wait_recv()
            total[...] += jnp.dot(attin[k, o], w_refs[k][...], preferred_element_type=f32)
        for way, behind in ((0, outer > 0), (1, outer < long - 1)):
            if not own:
                behind = behind & ((o > outer) if way == 0 else (o < outer))

            @pl.when(behind)
            def _():
                outer_copy(way, o).wait_recv()
                total[...] += rout[o + 1 - way].astype(f32)

        if not own:
            column[o] = total[...].astype(bf16)
            for way, ahead in ((0, o > outer), (1, o < outer)):
                @pl.when(ahead)
                def _():
                    outer_copy(way, o).start()

    def project_far(n, carry):
        project(order_of(n, place, long), False)
        return carry

    lax.fori_loop(0, long - 1, project_far, 0)
    project(outer, True)
    for k in range(1, groups):
        plan_copy(k).wait_recv()
    stream = (res_ref[...].astype(f32) + total[...]).astype(bf16)
    stream_ref[...] = stream
    wide = stream.astype(f32)
    all_ref[outer, inner] = (
        wide
        * lax.rsqrt(jnp.mean(wide * wide, axis=-1, keepdims=True) + 1e-06)
        * gain_ref[...]
    ).astype(bf16)

    def pass_on(way, o, i, lanes="all"):
        target = exp + (short, -short, 1, -1)[way]
        width = all_ref.shape[3]
        lower, upper = {"all": (0, width), "last": (0, width - direct), "direct": (width - direct, width)}[lanes]
        view = all_ref.at[o, i] if lanes == "all" else all_ref.at[o, i, :, lower:upper]
        sems = (bsend, brecv) if lanes == "direct" else (asend, arecv)
        return pltpu.make_async_remote_copy(
            src_ref=view,
            dst_ref=view,
            send_sem=sems[0].at[way, o, i],
            recv_sem=sems[1].at[o, i],
            device_id={"exp": target},
            device_id_type=MESH,
        )

    def to_column(k, o, i):
        target = (me + k) % columns
        return pltpu.make_async_remote_copy(
            src_ref=pack.at[o, i, target],
            dst_ref=arr_ref.at[o, me, i],
            send_sem=ysend.at[k, o, i],
            recv_sem=yrecv.at[k, o, i],
            device_id={"req": target},
            device_id_type=MESH,
        )

    def dispatch(o, i):
        taken = slots_of(plan_ref[o, i], exp, columns, groups, pack.shape[3])[1]
        select = jnp.concatenate([each.astype(f32) for each in taken], axis=0)
        rows = jnp.dot(
            select.astype(bf16), all_ref[o, i], preferred_element_type=f32
        ).astype(bf16)
        pack[o, i] = rows.reshape(pack.shape[2:])
        for k in range(1, columns):
            to_column(k, o, i).start()
        arr_ref[o, me, i] = pack[o, i, me]

    def onward(o, i, distance, side, lanes):
        for way, ahead in ((0, outer < long - 1), (1, outer > 0)):
            if distance == 0 or way == 1 - side:
                @pl.when(ahead)
                def _():
                    pass_on(way, o, i, lanes).start()

    def spread(o, distance, side):
        if distance > 0:
            pass_on(0, o, inner).wait_recv()
        onward(o, inner, distance, side, "all")
        for way, ahead in ((2, inner < short - 1), (3, inner > 0)):
            @pl.when(ahead)
            def _():
                pass_on(way, o, inner, "last" if direct and distance else "all").start()
        dispatch(o, inner)

    def across(o, distance, side):
        for gap in range(1, short):
            for way, i, ok, ahead in (
                (2, inner - gap, inner - gap >= 0, inner < short - 1),
                (3, inner + gap, inner + gap < short, inner > 0),
            ):
                @pl.when(ok)
                def _():
                    if direct and distance:
                        pass_on(0, o, i, "direct").wait_recv()
                        onward(o, i, distance, side, "direct")
                        pass_on(way, o, i, "last").wait_recv()
                    else:
                        pass_on(way, o, i).wait_recv()
                        if direct:
                            onward(o, i, distance, side, "direct")
                    if short > 2:
                        @pl.when(ahead)
                        def _():
                            pass_on(way, o, i).start()
                    dispatch(o, i)

    for step in range(long + 1):
        if step < long:
            near(place, long, step, spread)
        if step > 0:
            near(place, long, step - 1, across)

    for k in range(1, groups):
        plan_copy(k).wait_send()
    for o in range(long):
        for k in range(1, short):
            rows_copy(k, o).wait_send()

        @pl.when(outer < o)
        def _():
            outer_copy(0, o).wait_send()

        @pl.when(outer > o)
        def _():
            outer_copy(1, o).wait_send()

        for i in range(short):
            for lanes, there in (("all", inner == i), ("direct", inner != i)):
                if lanes == "all" or direct:
                    @pl.when(there & (outer >= o) & (outer < long - 1))
                    def _():
                        pass_on(0, o, i, lanes).wait_send()

                    @pl.when(there & (outer <= o) & (outer > 0))
                    def _():
                        pass_on(1, o, i, lanes).wait_send()

            for way, sent in (
                (2, (inner >= i) & (inner < short - 1)), (3, (inner <= i) & (inner > 0)),
            ):
                if direct:
                    @pl.when(sent & (inner == i) & (outer == o))
                    def _():
                        pass_on(way, o, i).wait_send()

                    @pl.when(sent & (inner == i) & (outer != o))
                    def _():
                        pass_on(way, o, i, "last").wait_send()
                else:
                    @pl.when(sent)
                    def _():
                        pass_on(way, o, i).wait_send()

            for k in range(1, columns):
                to_column(k, o, i).wait_send()
                to_column(k, o, i).wait_recv()


def near(place, long, distance, body):
    outer = place[0]

    @pl.when(outer + distance < long)
    def _():
        body(outer + distance, distance, 0)

    if distance > 0:
        @pl.when(outer - distance >= 0)
        def _():
            body(outer - distance, distance, 1)


def front(attended, out_weights, residual, norm_gain, plan, rows, line, columns):
    long, short = line
    tokens, width = residual.shape
    depth = out_weights[0].shape[0]
    dma = pltpu.SemaphoreType.DMA
    block = (long, short, tokens, width)
    vmem = pl.BlockSpec(memory_space=pltpu.VMEM)
    bf16 = jnp.bfloat16

    def kernel(att_ref, *refs):
        front_kernel(line, columns, att_ref, refs[:short], *refs[short:])

    return pl.pallas_call(
        kernel,
        out_shape=(
            jax.ShapeDtypeStruct((tokens, width), bf16),
            jax.ShapeDtypeStruct(block, bf16),
            jax.ShapeDtypeStruct((long, columns, short, rows, width), bf16),
            jax.ShapeDtypeStruct((long, short) + plan.shape, jnp.float32),
        ),
        in_specs=[vmem] * (4 + short),
        out_specs=(vmem, vmem, vmem, vmem),
        scratch_shapes=[
            pltpu.VMEM((short, long, tokens, depth), bf16),
            pltpu.VMEM((long, tokens, width), bf16),
            pltpu.VMEM((long + 1, tokens, width), bf16),
            pltpu.VMEM((tokens, width), jnp.float32),
            pltpu.VMEM((long, short, columns, rows, width), bf16),
            dma((short, long)),
            dma((short, long)),
            dma((2, long)),
            dma((2, long)),
            dma((4, long, short)),
            dma((long, short)),
            dma((4, long, short)),
            dma((long, short)),
            dma((columns, long, short)),
            dma((columns, long, short)),
            dma((long * short,)),
            dma((long * short,)),
        ],
        compiler_params=pltpu.CompilerParams(
            collective_id=0, has_side_effects=True, vmem_limit_bytes=56 * 2**20
        ),
        cost_estimate=pl.CostEstimate(
            flops=4 * 10**9, bytes_accessed=2 * 10**7, transcendentals=0
        ),
    )(
        attended.reshape(long, short, tokens, depth), *out_weights, residual,
        norm_gain.reshape(1, width), plan,
    )


def order_of(k, place, long):
    outer = place[0]
    low = jnp.where(2 * outer <= long - 1, outer, long - 1 - outer)
    skip = long - 1 - 2 * low
    pair = jnp.maximum(k - skip, 0)
    gap = low - pair // 2
    o = jnp.where(k < skip, long - 1 - k, low + gap * (1 - 2 * (pair % 2)))
    return jnp.where(2 * outer <= long - 1, o, long - 1 - o)


def tiles(width, step):
    return [(lower, min(lower + step, width)) for lower in range(0, width, step)]


def back_kernel(
    line, columns, arr_ref, all_ref, eg_ref, ed_ref, sg_ref, sd_ref, gate_ref, plan_ref,
    stream_ref, out_ref, rows, part, eg, ed, sg, sd, ret, rin, rout, column, total, hidden,
    shidden, sideout, sidecol, sidein, load, isend, irecv, osend, orecv, ysend, yrecv, ssend,
    srecv, tsend, trecv,
):
    long, short = line
    exp = lax.axis_index("exp")
    me = lax.axis_index("req")
    place = (exp // short, exp % short)
    outer, inner = place
    width = eg.shape[1]
    direct = sidecol.shape[2] if short == 2 else 0
    near_lanes = slice(0, width - direct)
    far_lanes = slice(width - direct, width)
    bf16, f32 = (jnp.bfloat16, jnp.float32)

    load_rows = pltpu.make_async_copy(arr_ref, rows, load.at[0])
    load_eg = pltpu.make_async_copy(eg_ref.at[0], eg, load.at[1])
    load_ed = pltpu.make_async_copy(ed_ref.at[0], ed, load.at[2])
    load_sg = pltpu.make_async_copy(sg_ref, sg, load.at[3])
    load_sd = pltpu.make_async_copy(sd_ref, sd, load.at[4])
    load_all = pltpu.make_async_copy(all_ref, part, load.at[5])
    for copy in (load_rows, load_eg, load_ed):
        copy.start()
    greet(place, line, long * short, columns, False)

    def answer_copy(k, o):
        target = (me + k) % columns
        return pltpu.make_async_remote_copy(
            src_ref=rows.at[o, target],
            dst_ref=ret.at[o, me],
            send_sem=ysend.at[k, o],
            recv_sem=yrecv.at[k, o],
            device_id={"req": target},
            device_id_type=MESH,
        )

    load_rows.wait()
    load_eg.wait()
    for copy in (load_all, load_sg, load_sd):
        copy.start()

    def expert(k):
        o = order_of(k, place, long)
        x = rows[o].reshape(hidden.shape[0], width)
        for lower, upper in tiles(eg.shape[2], 256):
            gate = jnp.dot(x, eg[0, :, lower:upper], preferred_element_type=f32)
            up = jnp.dot(x, eg[1, :, lower:upper], preferred_element_type=f32)
            hidden[:, lower:upper] = (jax.nn.silu(gate) * up).astype(bf16)

        @pl.when(k == 0)
        def _():
            load_ed.wait()

        for lower, upper in tiles(width, 512):
            down = jnp.dot(hidden[...], ed[:, lower:upper], preferred_element_type=f32)
            rows[o, :, :, :, lower:upper] = down.astype(bf16).reshape(
                rows.shape[1:4] + (upper - lower,)
            )
        for j in range(1, columns):
            answer_copy(j, o).start()
        ret[o, me] = rows[o, me]

    def inner_copy(way, o, i, relay):
        slot = rin.at[o, i + 1 - way]
        source = slot if relay else part.at[o, i]
        if direct:
            slot, source = slot.at[:, near_lanes], source.at[:, near_lanes]
        return pltpu.make_async_remote_copy(
            src_ref=source,
            dst_ref=slot,
            send_sem=isend.at[way, o, i],
            recv_sem=irecv.at[way, o, i],
            device_id={"exp": outer * short + inner + 1 - 2 * way},
            device_id_type=MESH,
        )

    def outer_copy(way, o):
        return pltpu.make_async_remote_copy(
            src_ref=column.at[o],
            dst_ref=rout.at[o + 1 - way],
            send_sem=osend.at[way, o],
            recv_sem=orecv.at[way, o],
            device_id={"exp": (outer + 1 - 2 * way) * short + inner},
            device_id_type=MESH,
        )

    def side_copy(way, o):
        return pltpu.make_async_remote_copy(
            src_ref=sidecol.at[o],
            dst_ref=sideout.at[o + 1 - way],
            send_sem=ssend.at[way, o],
            recv_sem=srecv.at[way, o],
            device_id={"exp": (outer + 1 - 2 * way) * short + inner},
            device_id_type=MESH,
        )

    def last_copy():
        return pltpu.make_async_remote_copy(
            src_ref=sidecol.at[outer],
            dst_ref=sidein,
            send_sem=tsend,
            recv_sem=trecv,
            device_id={"exp": outer * short + 1 - inner},
            device_id_type=MESH,
        )

    def side(o, own):
        value = part[o, 1 - inner, :, far_lanes].astype(f32)
        total[:, far_lanes] = value
        for way, behind in ((0, outer > 0), (1, outer < long - 1)):
            if not own:
                behind = behind & ((o > outer) if way == 0 else (o < outer))

            @pl.when(behind)
            def _():
                side_copy(way, o).wait_recv()
                total[:, far_lanes] += sideout[o + 1 - way].astype(f32)

        sidecol[o] = total[:, far_lanes].astype(bf16)
        if own:
            last_copy().start()
        else:
            for way, ahead in ((0, o > outer), (1, o < outer)):
                @pl.when(ahead)
                def _():
                    side_copy(way, o).start()

    def toward(way, gap):
        i = inner + gap * (1 - 2 * way)
        ok = (i < short) if way == 0 else (i >= 0)
        behind = (inner > 0) if way == 0 else (inner < short - 1)
        return i, ok, behind

    def fill(o):
        for i in range(short):
            x = part[o, i]
            scale = jax.nn.sigmoid(
                jnp.sum(x.astype(f32) * gate_ref[...].astype(f32), axis=-1, keepdims=True)
            )
            for lower, upper in tiles(sg.shape[1], 256):
                gate = lax.dot_general(
                    x, sg[0, lower:upper], ROWS_BY_ROWS, preferred_element_type=f32
                )
                up = lax.dot_general(
                    x, sg[1, lower:upper], ROWS_BY_ROWS, preferred_element_type=f32
                )
                shidden[:, lower:upper] = (jax.nn.silu(gate) * up).astype(bf16)
            for lower, upper in tiles(width, 512):
                down = jnp.dot(shidden[...], sd[:, lower:upper], preferred_element_type=f32)
                part[o, i, :, lower:upper] = (scale * down).astype(bf16)
        for j in range(1, columns):
            answer_copy(j, o).wait_recv()
        for i in range(short):
            hits, taken = slots_of(
                plan_ref[o, i], exp, columns, long * short, rows.shape[3]
            )
            weights = plan_ref[o, i, plan_ref.shape[2] // 2 :]
            spread = jnp.concatenate(
                [
                    jnp.where(
                        taken[c],
                        jnp.sum(
                            jnp.where(hits[c], weights, 0.0), axis=0, keepdims=True
                        ),
                        0.0,
                    )
                    for c in range(columns)
                ],
                axis=0,
            ).astype(bf16)
            for lower, upper in tiles(width, 512):
                picked = ret[o, :, i, :, lower:upper].reshape(-1, upper - lower)
                routed = lax.dot_general(
                    spread, picked, (((0,), (0,)), ((), ())), preferred_element_type=f32
                )
                part[o, i, :, lower:upper] = (
                    part[o, i, :, lower:upper].astype(f32) + routed
                ).astype(bf16)

    def first(o):
        fill(o)
        for way in (0, 1):
            for gap in range(short - 1, 0, -1):
                i, ok, behind = toward(way, gap)
                if short > 2:
                    ok = ok & jnp.logical_not(behind)

                @pl.when(ok)
                def _():
                    inner_copy(way, o, i, False).start()

    def second(o, own):
        if short > 2:
            for way in (0, 1):
                for gap in range(short - 1, 0, -1):
                    i, ok, behind = toward(way, gap)

                    @pl.when(ok & behind)
                    def _():
                        inner_copy(way, o, i, True).wait_recv()
                        slot = i + 1 - way
                        rin[o, slot] = (
                            rin[o, slot].astype(f32) + part[o, i].astype(f32)
                        ).astype(bf16)
                        inner_copy(way, o, i, True).start()

        if direct:
            side(o, own)
        total[...] = part[o, inner].astype(f32)
        for way, behind in ((0, inner > 0), (1, inner < short - 1)):
            @pl.when(behind)
            def _():
                inner_copy(way, o, inner, False).wait_recv()
                total[:, near_lanes] += rin[o, inner + 1 - way, :, near_lanes].astype(f32)

        for way, behind in ((0, outer > 0), (1, outer < long - 1)):
            if not own:
                behind = behind & ((o > outer) if way == 0 else (o < outer))

            @pl.when(behind)
            def _():
                outer_copy(way, o).wait_recv()
                total[...] += rout[o + 1 - way].astype(f32)

        if not own:
            column[o] = total[...].astype(bf16)
            for way, ahead in ((0, o > outer), (1, o < outer)):
                @pl.when(ahead)
                def _():
                    outer_copy(way, o).start()

    def step(k, carry):
        @pl.when(k < long)
        def _():
            expert(k)

        @pl.when(k == 1)
        def _():
            load_all.wait()
            load_sg.wait()
            load_sd.wait()

        @pl.when(k > 0)
        def _():
            first(order_of(k - 1, place, long))

        @pl.when(k > 1)
        def _():
            second(order_of(k - 2, place, long), False)

        return carry

    lax.fori_loop(0, long + 1, step, 0)
    second(outer, True)
    if direct:
        last_copy().wait_recv()
        total[:, far_lanes] += sidein[...].astype(f32)
        last_copy().wait_send()
    out_ref[...] = (stream_ref[...].astype(f32) + total[...]).astype(bf16)

    for o in range(long):
        for i in range(short):
            @pl.when(inner < i)
            def _():
                inner_copy(0, o, i, False).wait_send()

            @pl.when(inner > i)
            def _():
                inner_copy(1, o, i, False).wait_send()

        @pl.when(outer < o)
        def _():
            outer_copy(0, o).wait_send()
            if direct:
                side_copy(0, o).wait_send()

        @pl.when(outer > o)
        def _():
            outer_copy(1, o).wait_send()
            if direct:
                side_copy(1, o).wait_send()

        for j in range(1, columns):
            answer_copy(j, o).wait_send()


def back(
    arrived, gathered, expert_gate_up, expert_down, shared_gate_up, shared_down, shared_gate,
    plan, stream, line, columns,
):
    long, short = line
    tokens, width = stream.shape
    count = arrived.shape[3]
    direct = max(128, width // 8 // 128 * 128)
    hid, shid = (expert_down.shape[1], shared_down.shape[0])
    dma = pltpu.SemaphoreType.DMA
    block = (long, short, tokens, width)
    vmem = pl.BlockSpec(memory_space=pltpu.VMEM)
    hbm = pl.BlockSpec(memory_space=pl.ANY)
    bf16 = jnp.bfloat16
    return pl.pallas_call(
        functools.partial(back_kernel, line, columns),
        out_shape=jax.ShapeDtypeStruct((tokens, width), bf16),
        in_specs=[hbm] * 6 + [vmem] * 3,
        out_specs=vmem,
        scratch_shapes=[
            pltpu.VMEM(arrived.shape, bf16),
            pltpu.VMEM(block, bf16),
            pltpu.VMEM(expert_gate_up.shape[1:], bf16),
            pltpu.VMEM(expert_down.shape[1:], bf16),
            pltpu.VMEM(shared_gate_up.shape, bf16),
            pltpu.VMEM(shared_down.shape, bf16),
            pltpu.VMEM(arrived.shape, bf16),
            pltpu.VMEM((long, short + 1, tokens, width), bf16),
            pltpu.VMEM((long + 1, tokens, width), bf16),
            pltpu.VMEM((long, tokens, width), bf16),
            pltpu.VMEM((tokens, width), jnp.float32),
            pltpu.VMEM((columns * short * count, hid), bf16),
            pltpu.VMEM((tokens, shid), bf16),
            pltpu.VMEM((long + 1, tokens, direct), bf16),
            pltpu.VMEM((long, tokens, direct), bf16),
            pltpu.VMEM((tokens, direct), bf16),
            dma((6,)),
            dma((2, long, short)),
            dma((2, long, short)),
            dma((2, long)),
            dma((2, long)),
            dma((columns, long)),
            dma((columns, long)),
            dma((2, long)),
            dma((2, long)),
            dma,
            dma,
        ],
        compiler_params=pltpu.CompilerParams(
            collective_id=1, has_side_effects=True, vmem_limit_bytes=60 * 2**20
        ),
        cost_estimate=pl.CostEstimate(
            flops=3 * 10**10, bytes_accessed=5 * 10**7, transcendentals=0
        ),
    )(
        arrived, gathered, expert_gate_up, expert_down, shared_gate_up, shared_down,
        shared_gate.reshape(1, width), plan, stream,
    )


def on_device(
    residual,
    prefill_qkv,
    decode_qkv,
    cache_pool,
    page_table,
    cache_len,
    out_weight,
    norm_gain,
    shared_gate_up,
    shared_down,
    shared_gate,
    routes,
    route_weight,
    expert_gate_up,
    expert_down,
):
    groups = lax.axis_size("exp")
    columns = lax.axis_size("req")
    line = (LINE, groups // LINE)
    out_weights = [out_weight]
    for k in range(1, line[1]):
        turn = [
            (o * line[1] + i, o * line[1] + (i + k) % line[1])
            for o in range(line[0])
            for i in range(line[1])
        ]
        out_weights.append(lax.ppermute(out_weight, "exp", turn))
    attended = attend(prefill_qkv, decode_qkv, cache_pool, page_table, cache_len)
    plan = jnp.concatenate([routes.T.astype(jnp.float32), route_weight.T], axis=0)
    rows = row_limit(routes.shape, groups)
    stream, gathered, arrived, plan = front(
        attended, out_weights, residual, norm_gain, plan, rows, line, columns
    )
    return back(
        arrived, gathered, expert_gate_up, expert_down, jnp.swapaxes(shared_gate_up, 1, 2),
        shared_down, shared_gate, plan, stream, line, columns,
    )


def row_limit(routes_shape, groups):
    tok_rows, route_count = routes_shape
    return max(2, tok_rows * route_count * 2 // (EXP_COL * groups))


def solution(mesh):
    placed = (
        P(("req", "exp"), None),
        P("req", None, None, "exp"),
        P("req", None, "exp"),
        P(None, "req", None, "exp"),
        P("req", None),
        P("req"),
        P("exp", None),
        P(),
        P(None, None, "exp"),
        P("exp", None),
        P(),
        P(("req", "exp"), None),
        P(("req", "exp"), None),
        P(("req", "exp"), None, None, None),
        P(("req", "exp"), None, None),
    )
    return jax.shard_map(
        on_device, mesh=mesh, in_specs=placed, out_specs=P(("req", "exp"), None), check_vma=False
    )
```

```python
import functools

import jax
import jax.numpy as jnp
from jax import lax
from jax.experimental import pallas as pl
from jax.experimental.pallas import tpu as pltpu
from jax.sharding import PartitionSpec as P

HD = 128
EXP_COL = 4
ROW_TILE = 16


NEG_FILL = -1e30
ROWS_BY_ROWS = (((1,), (1,)), ((), ()))


def attention_kernel(
    heads, q_ref, k_ref, v_ref, dq_ref, dk_ref, dv_ref, code_ref, ck_ref, cv_ref, out_ref,
    high_ref, sum_ref, acc_ref,
):
    step = pl.program_id(0)
    scaling = HD ** (-0.5)
    span_len = q_ref.shape[2]
    requests, width = dq_ref.shape
    rows = heads * requests

    query, keys, values = (q_ref[0, 0], k_ref[0, 0], v_ref[0, 0])
    half = span_len // 2
    base = pl.multiple_of((step // heads) * span_len, span_len)
    lane = pl.multiple_of((step % heads) * HD, HD)
    for lower, upper in ((0, half), (half, span_len)):
        scores = lax.dot_general(
            query[lower:upper], keys[:upper], ROWS_BY_ROWS, preferred_element_type=jnp.float32
        ) * scaling
        row = lax.broadcasted_iota(jnp.int32, scores.shape, 0) + lower
        column = lax.broadcasted_iota(jnp.int32, scores.shape, 1)
        scores = jnp.where(row >= column, scores, NEG_FILL)
        raised = jnp.exp(scores - jnp.max(scores, axis=-1, keepdims=True))
        total = jnp.sum(raised, axis=-1, keepdims=True)
        mixed = jnp.dot(
            raised.astype(jnp.bfloat16), values[:upper], preferred_element_type=jnp.float32
        )
        out_ref[pl.ds(base + lower, upper - lower), pl.ds(lane, HD)] = (mixed / total).astype(
            out_ref.dtype
        )

    head_of = lax.broadcasted_iota(jnp.int32, (rows, width), 0) // requests
    lane_head = lax.broadcasted_iota(jnp.int32, (rows, width), 1) // HD
    queries = jnp.where(
        head_of == lane_head,
        jnp.concatenate([dq_ref[...].astype(jnp.float32)] * heads, axis=0),
        0.0,
    )

    @pl.when(step == 0)
    def _():
        own = jnp.concatenate([dk_ref[...].astype(jnp.float32)] * heads, axis=0)
        high_ref[...] = jnp.sum(queries * own, axis=-1, keepdims=True) * scaling
        sum_ref[...] = jnp.ones_like(sum_ref)
        acc_ref[...] = jnp.concatenate([dv_ref[...].astype(jnp.float32)] * heads, axis=0)

    scores = lax.dot_general(
        queries.astype(jnp.bfloat16), ck_ref[0], ROWS_BY_ROWS, preferred_element_type=jnp.float32
    ) * scaling
    request = lax.broadcasted_iota(jnp.int32, scores.shape, 0) % requests
    allowed = request == code_ref[...]
    scores = jnp.where(allowed, scores, NEG_FILL)
    before = high_ref[...]
    after = jnp.maximum(before, jnp.max(scores, axis=-1, keepdims=True))
    raised = jnp.where(allowed, jnp.exp(scores - after), 0.0)
    fade = jnp.exp(before - after)
    high_ref[...] = after
    sum_ref[...] = sum_ref[...] * fade + jnp.sum(raised, axis=-1, keepdims=True)
    acc_ref[...] = acc_ref[...] * fade + jnp.dot(
        raised.astype(jnp.bfloat16), cv_ref[0], preferred_element_type=jnp.float32
    )

    @pl.when(step == pl.num_programs(0) - 1)
    def _():
        mixed = acc_ref[...] / sum_ref[...]
        first = out_ref.shape[0] - requests
        for head in range(heads):
            lanes = slice(head * HD, (head + 1) * HD)
            out_ref[first:, lanes] = mixed[
                head * requests : (head + 1) * requests, lanes
            ].astype(out_ref.dtype)


def attend(prefill_qkv, decode_qkv, cache_pool, page_table, cache_len):
    spans, _, span_len, width = prefill_qkv.shape
    requests = decode_qkv.shape[0]
    heads = width // HD
    steps = spans * heads
    pool_pages, page_len = (cache_pool.shape[1], cache_pool.shape[2])
    max_pages = page_table.shape[1]
    chunk = pool_pages // steps * page_len
    order = jnp.arange(max_pages, dtype=jnp.int32)
    left = cache_len[:, None] - order[None, :] * page_len
    held = (page_table[None] == jnp.arange(pool_pages, dtype=jnp.int32)[:, None, None]) & (
        left > 0
    )[None]
    owner = jnp.max(
        jnp.where(held, jnp.arange(requests, dtype=jnp.int32)[None, :, None], -1), axis=(1, 2)
    )
    valid = jnp.max(jnp.where(held, left[None], 0), axis=(1, 2))
    code = jnp.where(
        jnp.arange(page_len, dtype=jnp.int32)[None, :] < valid[:, None], owner[:, None], -1
    ).reshape(1, pool_pages * page_len)
    pool = cache_pool.reshape(2, pool_pages * page_len, width)
    whole = pl.BlockSpec((requests, width), lambda g: (0, 0))
    part = [
        pl.BlockSpec((1, 1, span_len, HD), functools.partial(lambda j, g: (g // heads, j, 0, g % heads), j))
        for j in range(3)
    ]
    out_rows = spans * span_len + requests
    return pl.pallas_call(
        functools.partial(attention_kernel, heads),
        grid=(steps,),
        in_specs=part
        + [whole] * 3
        + [
            pl.BlockSpec((1, chunk), lambda g: (0, g)),
            pl.BlockSpec((1, chunk, width), lambda g: (0, g, 0)),
            pl.BlockSpec((1, chunk, width), lambda g: (1, g, 0)),
        ],
        out_specs=pl.BlockSpec((out_rows, width), lambda g: (0, 0)),
        out_shape=jax.ShapeDtypeStruct((out_rows, width), jnp.bfloat16),
        scratch_shapes=[
            pltpu.VMEM((heads * requests, 1), jnp.float32),
            pltpu.VMEM((heads * requests, 1), jnp.float32),
            pltpu.VMEM((heads * requests, width), jnp.float32),
        ],
        compiler_params=pltpu.CompilerParams(vmem_limit_bytes=40 * 2**20),
        cost_estimate=pl.CostEstimate(
            flops=2 * 10**9, bytes_accessed=2 * pool.size + 2 * prefill_qkv.size, transcendentals=2 * 10**6
        ),
    )(
        prefill_qkv, prefill_qkv, prefill_qkv,
        decode_qkv[:, 0], decode_qkv[:, 1], decode_qkv[:, 2],
        code, pool, pool,
    )


LINE = 4
MESH = pl.DeviceIdType.MESH


def greet(place, line, groups, columns, all_groups):
    outer, inner = place
    long, short = line
    barrier = pltpu.get_barrier_semaphore()
    count = jnp.int32(0)
    if all_groups:
        exp = outer * short + inner
        for k in range(1, groups):
            pl.semaphore_signal(
                barrier, inc=1, device_id={"exp": (exp + k) % groups}, device_id_type=MESH
            )
        count = count + (groups - 1)
    for ok, target in () if all_groups else (
        (outer > 0, (outer - 1) * short + inner),
        (outer < long - 1, (outer + 1) * short + inner),
        (inner > 0, outer * short + inner - 1),
        (inner < short - 1, outer * short + inner + 1),
    ):
        @pl.when(ok)
        def _():
            pl.semaphore_signal(barrier, inc=1, device_id={"exp": target}, device_id_type=MESH)

        count = count + ok.astype(jnp.int32)
    if columns > 1:
        me = lax.axis_index("req")
        for k in range(1, columns):
            pl.semaphore_signal(
                barrier, inc=1, device_id={"req": (me + k) % columns}, device_id_type=MESH
            )
        count = count + (columns - 1)
    pl.semaphore_wait(barrier, count)


def slots_of(plan, exp, columns, groups, rows):
    tokens = plan.shape[1]
    routes = plan[: plan.shape[0] // 2]
    halves = columns // EXP_COL
    hits = [
        routes == ((c * groups + exp) // halves).astype(jnp.float32) for c in range(columns)
    ]
    named = jnp.concatenate(
        [jnp.max(hit.astype(jnp.float32), axis=0, keepdims=True) for hit in hits], axis=0
    )
    upto = lax.broadcasted_iota(jnp.int32, (tokens, tokens), 0) <= lax.broadcasted_iota(
        jnp.int32, (tokens, tokens), 1
    )
    rank = jnp.dot(
        named.astype(jnp.bfloat16), upto.astype(jnp.bfloat16), preferred_element_type=jnp.float32
    )
    rank = jnp.where(named > 0.0, rank - 1.0, -1.0).astype(jnp.int32)
    slot = lax.broadcasted_iota(jnp.int32, (rows, tokens), 0)
    return hits, [slot == rank[c : c + 1] for c in range(columns)]


def front_kernel(
    line, columns, att_ref, w_refs, res_ref, gain_ref, mine_ref, gate_ref, sg_ref, sd_ref,
    stream_ref, shared_ref, arr_ref, plan_ref, all_ref, sg, sd, shidden, load, attin, column, rout, total, pack, isend, irecv, osend, orecv, asend, arecv, bsend,
    brecv, ysend, yrecv, psend, precv,
):
    long, short = line
    groups = long * short
    exp = lax.axis_index("exp")
    me = lax.axis_index("req")
    place = (exp // short, exp % short)
    outer, inner = place
    f32, bf16 = (jnp.float32, jnp.bfloat16)
    direct = all_ref.shape[3] // 8 // 128 * 128 if short == 2 else 0
    load_sg = pltpu.make_async_copy(sg_ref, sg, load.at[0])
    load_sd = pltpu.make_async_copy(sd_ref, sd, load.at[1])
    load_sg.start()
    load_sd.start()
    greet(place, line, groups, columns, True)

    def rows_copy(k, o):
        target = (inner + k) % short
        return pltpu.make_async_remote_copy(
            src_ref=att_ref.at[o, target],
            dst_ref=attin.at[k, o],
            send_sem=isend.at[k, o],
            recv_sem=irecv.at[k, o],
            device_id={"exp": outer * short + target},
            device_id_type=MESH,
        )

    def outer_copy(way, o):
        return pltpu.make_async_remote_copy(
            src_ref=column.at[o],
            dst_ref=rout.at[o + 1 - way],
            send_sem=osend.at[way, o],
            recv_sem=orecv.at[way, o],
            device_id={"exp": (outer + 1 - 2 * way) * short + inner},
            device_id_type=MESH,
        )

    def plan_copy(k):
        return pltpu.make_async_remote_copy(
            src_ref=mine_ref,
            dst_ref=plan_ref.at[outer, inner],
            send_sem=psend.at[k],
            recv_sem=precv.at[k],
            device_id={"exp": (exp + k) % groups},
            device_id_type=MESH,
        )

    def send_rows(n, carry):
        for k in range(1, short):
            rows_copy(k, order_of(n, place, long)).start()
        return carry

    lax.fori_loop(0, long, send_rows, 0)
    for k in range(1, groups):
        plan_copy(k).start()
    plan_ref[outer, inner] = mine_ref[...]

    def project(o, own):
        total[...] = jnp.dot(att_ref[o, inner], w_refs[0][...], preferred_element_type=f32)
        for k in range(1, short):
            rows_copy(k, o).wait_recv()
            total[...] += jnp.dot(attin[k, o], w_refs[k][...], preferred_element_type=f32)
        for way, behind in ((0, outer > 0), (1, outer < long - 1)):
            if not own:
                behind = behind & ((o > outer) if way == 0 else (o < outer))

            @pl.when(behind)
            def _():
                outer_copy(way, o).wait_recv()
                total[...] += rout[o + 1 - way].astype(f32)

        if not own:
            column[o] = total[...].astype(bf16)
            for way, ahead in ((0, o > outer), (1, o < outer)):
                @pl.when(ahead)
                def _():
                    outer_copy(way, o).start()

    def project_far(n, carry):
        project(order_of(n, place, long), False)
        return carry

    lax.fori_loop(0, long - 1, project_far, 0)
    project(outer, True)
    for k in range(1, groups):
        plan_copy(k).wait_recv()
    stream = (res_ref[...].astype(f32) + total[...]).astype(bf16)
    stream_ref[...] = stream
    wide = stream.astype(f32)
    all_ref[outer, inner] = (
        wide
        * lax.rsqrt(jnp.mean(wide * wide, axis=-1, keepdims=True) + 1e-06)
        * gain_ref[...]
    ).astype(bf16)

    def pass_on(way, o, i, lanes="all"):
        target = exp + (short, -short, 1, -1)[way]
        width = all_ref.shape[3]
        lower, upper = {"all": (0, width), "last": (0, width - direct), "direct": (width - direct, width)}[lanes]
        view = all_ref.at[o, i] if lanes == "all" else all_ref.at[o, i, :, lower:upper]
        sems = (bsend, brecv) if lanes == "direct" else (asend, arecv)
        return pltpu.make_async_remote_copy(
            src_ref=view,
            dst_ref=view,
            send_sem=sems[0].at[way, o, i],
            recv_sem=sems[1].at[o, i],
            device_id={"exp": target},
            device_id_type=MESH,
        )

    def to_column(k, o, i):
        target = (me + k) % columns
        return pltpu.make_async_remote_copy(
            src_ref=pack.at[o, i, target],
            dst_ref=arr_ref.at[o, me, i],
            send_sem=ysend.at[k, o, i],
            recv_sem=yrecv.at[k, o, i],
            device_id={"req": target},
            device_id_type=MESH,
        )

    def dispatch(o, i):
        taken = slots_of(plan_ref[o, i], exp, columns, groups, pack.shape[3])[1]
        select = jnp.concatenate([each.astype(f32) for each in taken], axis=0)
        rows = jnp.dot(
            select.astype(bf16), all_ref[o, i], preferred_element_type=f32
        ).astype(bf16)
        pack[o, i] = rows.reshape(pack.shape[2:])
        for k in range(1, columns):
            to_column(k, o, i).start()
        arr_ref[o, me, i] = pack[o, i, me]

    def shared(i, o):
        x = all_ref[o, i]
        scale = jax.nn.sigmoid(
            jnp.sum(x.astype(f32) * gate_ref[...].astype(f32), axis=-1, keepdims=True)
        )
        for lower, upper in tiles(sg.shape[1], 256):
            gate = lax.dot_general(
                x, sg[0, lower:upper], ROWS_BY_ROWS, preferred_element_type=f32
            )
            up = lax.dot_general(
                x, sg[1, lower:upper], ROWS_BY_ROWS, preferred_element_type=f32
            )
            shidden[:, lower:upper] = (jax.nn.silu(gate) * up).astype(bf16)
        for lower, upper in tiles(all_ref.shape[3], 512):
            down = jnp.dot(shidden[...], sd[:, lower:upper], preferred_element_type=f32)
            shared_ref[o, i, :, lower:upper] = (scale * down).astype(bf16)

    def share(o, distance, side):
        def one(i, carry):
            shared(i, o)
            return carry

        lax.fori_loop(0, short, one, 0)

    def onward(o, i, distance, side, lanes):
        for way, ahead in ((0, outer < long - 1), (1, outer > 0)):
            if distance == 0 or way == 1 - side:
                @pl.when(ahead)
                def _():
                    pass_on(way, o, i, lanes).start()

    def spread(o, distance, side):
        if distance > 0:
            pass_on(0, o, inner).wait_recv()
        onward(o, inner, distance, side, "all")
        for way, ahead in ((2, inner < short - 1), (3, inner > 0)):
            @pl.when(ahead)
            def _():
                pass_on(way, o, inner, "last" if direct and distance else "all").start()
        dispatch(o, inner)

    def across(o, distance, side):
        for gap in range(1, short):
            for way, i, ok, ahead in (
                (2, inner - gap, inner - gap >= 0, inner < short - 1),
                (3, inner + gap, inner + gap < short, inner > 0),
            ):
                @pl.when(ok)
                def _():
                    if direct and distance:
                        pass_on(0, o, i, "direct").wait_recv()
                        onward(o, i, distance, side, "direct")
                        pass_on(way, o, i, "last").wait_recv()
                    else:
                        pass_on(way, o, i).wait_recv()
                        if direct:
                            onward(o, i, distance, side, "direct")
                    if short > 2:
                        @pl.when(ahead)
                        def _():
                            pass_on(way, o, i).start()
                    dispatch(o, i)

    for step in range(long + 1):
        if step < long:
            near(place, long, step, spread)
        if step > 0:
            near(place, long, step - 1, across)
        if step == 1:
            load_sg.wait()
            load_sd.wait()
        if step > 1:
            near(place, long, step - 2, share)
    near(place, long, long - 1, share)

    for k in range(1, groups):
        plan_copy(k).wait_send()
    for o in range(long):
        for k in range(1, short):
            rows_copy(k, o).wait_send()

        @pl.when(outer < o)
        def _():
            outer_copy(0, o).wait_send()

        @pl.when(outer > o)
        def _():
            outer_copy(1, o).wait_send()

        for i in range(short):
            for lanes, there in (("all", inner == i), ("direct", inner != i)):
                if lanes == "all" or direct:
                    @pl.when(there & (outer >= o) & (outer < long - 1))
                    def _():
                        pass_on(0, o, i, lanes).wait_send()

                    @pl.when(there & (outer <= o) & (outer > 0))
                    def _():
                        pass_on(1, o, i, lanes).wait_send()

            for way, sent in (
                (2, (inner >= i) & (inner < short - 1)), (3, (inner <= i) & (inner > 0)),
            ):
                if direct:
                    @pl.when(sent & (inner == i) & (outer == o))
                    def _():
                        pass_on(way, o, i).wait_send()

                    @pl.when(sent & (inner == i) & (outer != o))
                    def _():
                        pass_on(way, o, i, "last").wait_send()
                else:
                    @pl.when(sent)
                    def _():
                        pass_on(way, o, i).wait_send()

            for k in range(1, columns):
                to_column(k, o, i).wait_send()
                to_column(k, o, i).wait_recv()


def near(place, long, distance, body):
    outer = place[0]

    @pl.when(outer + distance < long)
    def _():
        body(outer + distance, distance, 0)

    if distance > 0:
        @pl.when(outer - distance >= 0)
        def _():
            body(outer - distance, distance, 1)


def front(
    attended, out_weights, residual, norm_gain, plan, shared_gate_up, shared_down, shared_gate,
    rows, line, columns,
):
    long, short = line
    tokens, width = residual.shape
    depth = out_weights[0].shape[0]
    dma = pltpu.SemaphoreType.DMA
    block = (long, short, tokens, width)
    vmem = pl.BlockSpec(memory_space=pltpu.VMEM)
    bf16 = jnp.bfloat16

    def kernel(att_ref, *refs):
        front_kernel(line, columns, att_ref, refs[:short], *refs[short:])

    return pl.pallas_call(
        kernel,
        out_shape=(
            jax.ShapeDtypeStruct((tokens, width), bf16),
            jax.ShapeDtypeStruct(block, bf16),
            jax.ShapeDtypeStruct((long, columns, short, rows, width), bf16),
            jax.ShapeDtypeStruct((long, short) + plan.shape, jnp.float32),
        ),
        in_specs=[vmem] * (5 + short) + [pl.BlockSpec(memory_space=pl.ANY)] * 2,
        out_specs=(vmem, vmem, vmem, vmem),
        scratch_shapes=[
            pltpu.VMEM(block, bf16),
            pltpu.VMEM(shared_gate_up.shape, bf16),
            pltpu.VMEM(shared_down.shape, bf16),
            pltpu.VMEM((tokens, shared_down.shape[0]), bf16),
            dma((2,)),
            pltpu.VMEM((short, long, tokens, depth), bf16),
            pltpu.VMEM((long, tokens, width), bf16),
            pltpu.VMEM((long + 1, tokens, width), bf16),
            pltpu.VMEM((tokens, width), jnp.float32),
            pltpu.VMEM((long, short, columns, rows, width), bf16),
            dma((short, long)),
            dma((short, long)),
            dma((2, long)),
            dma((2, long)),
            dma((4, long, short)),
            dma((long, short)),
            dma((4, long, short)),
            dma((long, short)),
            dma((columns, long, short)),
            dma((columns, long, short)),
            dma((long * short,)),
            dma((long * short,)),
        ],
        compiler_params=pltpu.CompilerParams(
            collective_id=0, has_side_effects=True, vmem_limit_bytes=56 * 2**20
        ),
        cost_estimate=pl.CostEstimate(
            flops=4 * 10**9, bytes_accessed=2 * 10**7, transcendentals=0
        ),
    )(
        attended.reshape(long, short, tokens, depth), *out_weights, residual,
        norm_gain.reshape(1, width), plan, shared_gate.reshape(1, width), shared_gate_up,
        shared_down,
    )


def order_of(k, place, long):
    outer = place[0]
    low = jnp.where(2 * outer <= long - 1, outer, long - 1 - outer)
    skip = long - 1 - 2 * low
    pair = jnp.maximum(k - skip, 0)
    gap = low - pair // 2
    o = jnp.where(k < skip, long - 1 - k, low + gap * (1 - 2 * (pair % 2)))
    return jnp.where(2 * outer <= long - 1, o, long - 1 - o)


def tiles(width, step):
    return [(lower, min(lower + step, width)) for lower in range(0, width, step)]


def back_kernel(
    line, columns, arr_ref, shared_ref, eg_ref, ed_ref, plan_ref, stream_ref, out_ref, rows, part,
    eg, ed, ret, rin, rout, column, total, hidden, sideout, sidecol, sidein, load, isend, irecv, osend, orecv, ysend, yrecv, ssend,
    srecv, tsend, trecv,
):
    long, short = line
    exp = lax.axis_index("exp")
    me = lax.axis_index("req")
    place = (exp // short, exp % short)
    outer, inner = place
    width = eg.shape[1]
    direct = sidecol.shape[2] if short == 2 else 0
    near_lanes = slice(0, width - direct)
    far_lanes = slice(width - direct, width)
    bf16, f32 = (jnp.bfloat16, jnp.float32)

    cuts = tiles(eg.shape[2], 256)

    def load_rows(k):
        o = order_of(k, place, long)
        return pltpu.make_async_copy(arr_ref.at[o], rows.at[o], load.at[2 + k])

    def load_eg(t):
        lanes = slice(*cuts[t])
        return pltpu.make_async_copy(
            eg_ref.at[0, :, :, lanes], eg.at[:, :, lanes], load.at[2 + long + t]
        )

    load_ed = pltpu.make_async_copy(ed_ref.at[0], ed, load.at[0])
    load_shared = pltpu.make_async_copy(shared_ref, part, load.at[1])
    load_rows(0).start()
    for t in range(len(cuts)):
        load_eg(t).start()
    load_ed.start()
    for k in range(1, long):
        load_rows(k).start()
    load_shared.start()
    greet(place, line, long * short, columns, False)

    def answer_copy(k, o):
        target = (me + k) % columns
        return pltpu.make_async_remote_copy(
            src_ref=rows.at[o, target],
            dst_ref=ret.at[o, me],
            send_sem=ysend.at[k, o],
            recv_sem=yrecv.at[k, o],
            device_id={"req": target},
            device_id_type=MESH,
        )

    def expert(k):
        o = order_of(k, place, long)
        load_rows(k).wait()
        x = rows[o].reshape(hidden.shape[0], width)
        for t, (lower, upper) in enumerate(cuts):
            @pl.when(k == 0)
            def _():
                load_eg(t).wait()

            gate = jnp.dot(x, eg[0, :, lower:upper], preferred_element_type=f32)
            up = jnp.dot(x, eg[1, :, lower:upper], preferred_element_type=f32)
            hidden[:, lower:upper] = (jax.nn.silu(gate) * up).astype(bf16)

        @pl.when(k == 0)
        def _():
            load_ed.wait()

        for lower, upper in tiles(width, 512):
            down = jnp.dot(hidden[...], ed[:, lower:upper], preferred_element_type=f32)
            rows[o, :, :, :, lower:upper] = down.astype(bf16).reshape(
                rows.shape[1:4] + (upper - lower,)
            )
        for j in range(1, columns):
            answer_copy(j, o).start()
        ret[o, me] = rows[o, me]

    def inner_copy(way, o, i, relay):
        slot = rin.at[o, i + 1 - way]
        source = slot if relay else part.at[o, i]
        if direct:
            slot, source = slot.at[:, near_lanes], source.at[:, near_lanes]
        return pltpu.make_async_remote_copy(
            src_ref=source,
            dst_ref=slot,
            send_sem=isend.at[way, o, i],
            recv_sem=irecv.at[way, o, i],
            device_id={"exp": outer * short + inner + 1 - 2 * way},
            device_id_type=MESH,
        )

    def outer_copy(way, o):
        return pltpu.make_async_remote_copy(
            src_ref=column.at[o],
            dst_ref=rout.at[o + 1 - way],
            send_sem=osend.at[way, o],
            recv_sem=orecv.at[way, o],
            device_id={"exp": (outer + 1 - 2 * way) * short + inner},
            device_id_type=MESH,
        )

    def side_copy(way, o):
        return pltpu.make_async_remote_copy(
            src_ref=sidecol.at[o],
            dst_ref=sideout.at[o + 1 - way],
            send_sem=ssend.at[way, o],
            recv_sem=srecv.at[way, o],
            device_id={"exp": (outer + 1 - 2 * way) * short + inner},
            device_id_type=MESH,
        )

    def last_copy():
        return pltpu.make_async_remote_copy(
            src_ref=sidecol.at[outer],
            dst_ref=sidein,
            send_sem=tsend,
            recv_sem=trecv,
            device_id={"exp": outer * short + 1 - inner},
            device_id_type=MESH,
        )

    def side(o, own):
        value = part[o, 1 - inner, :, far_lanes].astype(f32)
        total[:, far_lanes] = value
        for way, behind in ((0, outer > 0), (1, outer < long - 1)):
            if not own:
                behind = behind & ((o > outer) if way == 0 else (o < outer))

            @pl.when(behind)
            def _():
                side_copy(way, o).wait_recv()
                total[:, far_lanes] += sideout[o + 1 - way].astype(f32)

        sidecol[o] = total[:, far_lanes].astype(bf16)
        if own:
            last_copy().start()
        else:
            for way, ahead in ((0, o > outer), (1, o < outer)):
                @pl.when(ahead)
                def _():
                    side_copy(way, o).start()

    def toward(way, gap):
        i = inner + gap * (1 - 2 * way)
        ok = (i < short) if way == 0 else (i >= 0)
        behind = (inner > 0) if way == 0 else (inner < short - 1)
        return i, ok, behind

    def fill(o):
        for j in range(1, columns):
            answer_copy(j, o).wait_recv()
        for i in range(short):
            hits, taken = slots_of(
                plan_ref[o, i], exp, columns, long * short, rows.shape[3]
            )
            weights = plan_ref[o, i, plan_ref.shape[2] // 2 :]
            spread = jnp.concatenate(
                [
                    jnp.where(
                        taken[c],
                        jnp.sum(
                            jnp.where(hits[c], weights, 0.0), axis=0, keepdims=True
                        ),
                        0.0,
                    )
                    for c in range(columns)
                ],
                axis=0,
            ).astype(bf16)
            for lower, upper in tiles(width, 512):
                picked = ret[o, :, i, :, lower:upper].reshape(-1, upper - lower)
                routed = lax.dot_general(
                    spread, picked, (((0,), (0,)), ((), ())), preferred_element_type=f32
                )
                part[o, i, :, lower:upper] = (
                    part[o, i, :, lower:upper].astype(f32) + routed
                ).astype(bf16)

    def first(o):
        fill(o)
        for way in (0, 1):
            for gap in range(short - 1, 0, -1):
                i, ok, behind = toward(way, gap)
                if short > 2:
                    ok = ok & jnp.logical_not(behind)

                @pl.when(ok)
                def _():
                    inner_copy(way, o, i, False).start()

    def second(o, own):
        if short > 2:
            for way in (0, 1):
                for gap in range(short - 1, 0, -1):
                    i, ok, behind = toward(way, gap)

                    @pl.when(ok & behind)
                    def _():
                        inner_copy(way, o, i, True).wait_recv()
                        slot = i + 1 - way
                        rin[o, slot] = (
                            rin[o, slot].astype(f32) + part[o, i].astype(f32)
                        ).astype(bf16)
                        inner_copy(way, o, i, True).start()

        if direct:
            side(o, own)
        total[...] = part[o, inner].astype(f32)
        for way, behind in ((0, inner > 0), (1, inner < short - 1)):
            @pl.when(behind)
            def _():
                inner_copy(way, o, inner, False).wait_recv()
                total[:, near_lanes] += rin[o, inner + 1 - way, :, near_lanes].astype(f32)

        for way, behind in ((0, outer > 0), (1, outer < long - 1)):
            if not own:
                behind = behind & ((o > outer) if way == 0 else (o < outer))

            @pl.when(behind)
            def _():
                outer_copy(way, o).wait_recv()
                total[...] += rout[o + 1 - way].astype(f32)

        if not own:
            column[o] = total[...].astype(bf16)
            for way, ahead in ((0, o > outer), (1, o < outer)):
                @pl.when(ahead)
                def _():
                    outer_copy(way, o).start()

    def step(k, carry):
        @pl.when(k < long)
        def _():
            expert(k)

        @pl.when(k == 1)
        def _():
            load_shared.wait()

        @pl.when(k > 0)
        def _():
            first(order_of(k - 1, place, long))

        @pl.when(k > 1)
        def _():
            second(order_of(k - 2, place, long), False)

        return carry

    lax.fori_loop(0, long + 1, step, 0)
    second(outer, True)
    if direct:
        last_copy().wait_recv()
        total[:, far_lanes] += sidein[...].astype(f32)
        last_copy().wait_send()
    out_ref[...] = (stream_ref[...].astype(f32) + total[...]).astype(bf16)

    for o in range(long):
        for i in range(short):
            @pl.when(inner < i)
            def _():
                inner_copy(0, o, i, False).wait_send()

            @pl.when(inner > i)
            def _():
                inner_copy(1, o, i, False).wait_send()

        @pl.when(outer < o)
        def _():
            outer_copy(0, o).wait_send()
            if direct:
                side_copy(0, o).wait_send()

        @pl.when(outer > o)
        def _():
            outer_copy(1, o).wait_send()
            if direct:
                side_copy(1, o).wait_send()

        for j in range(1, columns):
            answer_copy(j, o).wait_send()


def back(
    arrived, shared, expert_gate_up, expert_down, plan, stream, line, columns,
):
    long, short = line
    tokens, width = stream.shape
    count = arrived.shape[3]
    direct = max(128, width // 8 // 128 * 128)
    hid = expert_down.shape[1]
    dma = pltpu.SemaphoreType.DMA
    block = (long, short, tokens, width)
    vmem = pl.BlockSpec(memory_space=pltpu.VMEM)
    hbm = pl.BlockSpec(memory_space=pl.ANY)
    bf16 = jnp.bfloat16
    return pl.pallas_call(
        functools.partial(back_kernel, line, columns),
        out_shape=jax.ShapeDtypeStruct((tokens, width), bf16),
        in_specs=[hbm] * 4 + [vmem] * 2,
        out_specs=vmem,
        scratch_shapes=[
            pltpu.VMEM(arrived.shape, bf16),
            pltpu.VMEM(block, bf16),
            pltpu.VMEM(expert_gate_up.shape[1:], bf16),
            pltpu.VMEM(expert_down.shape[1:], bf16),
            pltpu.VMEM(arrived.shape, bf16),
            pltpu.VMEM((long, short + 1, tokens, width), bf16),
            pltpu.VMEM((long + 1, tokens, width), bf16),
            pltpu.VMEM((long, tokens, width), bf16),
            pltpu.VMEM((tokens, width), jnp.float32),
            pltpu.VMEM((columns * short * count, hid), bf16),
            pltpu.VMEM((long + 1, tokens, direct), bf16),
            pltpu.VMEM((long, tokens, direct), bf16),
            pltpu.VMEM((tokens, direct), bf16),
            dma((2 + long + len(tiles(hid, 256)),)),
            dma((2, long, short)),
            dma((2, long, short)),
            dma((2, long)),
            dma((2, long)),
            dma((columns, long)),
            dma((columns, long)),
            dma((2, long)),
            dma((2, long)),
            dma,
            dma,
        ],
        compiler_params=pltpu.CompilerParams(
            collective_id=1, has_side_effects=True, vmem_limit_bytes=60 * 2**20
        ),
        cost_estimate=pl.CostEstimate(
            flops=3 * 10**10, bytes_accessed=5 * 10**7, transcendentals=0
        ),
    )(
        arrived, shared, expert_gate_up, expert_down, plan, stream,
    )


def on_device(
    residual,
    prefill_qkv,
    decode_qkv,
    cache_pool,
    page_table,
    cache_len,
    out_weight,
    norm_gain,
    shared_gate_up,
    shared_down,
    shared_gate,
    routes,
    route_weight,
    expert_gate_up,
    expert_down,
):
    groups = lax.axis_size("exp")
    columns = lax.axis_size("req")
    line = (LINE, groups // LINE)
    out_weights = [out_weight]
    for k in range(1, line[1]):
        turn = [
            (o * line[1] + i, o * line[1] + (i + k) % line[1])
            for o in range(line[0])
            for i in range(line[1])
        ]
        out_weights.append(lax.ppermute(out_weight, "exp", turn))
    attended = attend(prefill_qkv, decode_qkv, cache_pool, page_table, cache_len)
    plan = jnp.concatenate([routes.T.astype(jnp.float32), route_weight.T], axis=0)
    rows = row_limit(routes.shape, groups)
    stream, shared, arrived, plan = front(
        attended, out_weights, residual, norm_gain, plan, jnp.swapaxes(shared_gate_up, 1, 2),
        shared_down, shared_gate, rows, line, columns,
    )
    return back(
        arrived, shared, expert_gate_up, expert_down, plan, stream, line, columns
    )


def row_limit(routes_shape, groups):
    tok_rows, route_count = routes_shape
    return max(2, tok_rows * route_count * 2 // (EXP_COL * groups))


def solution(mesh):
    placed = (
        P(("req", "exp"), None),
        P("req", None, None, "exp"),
        P("req", None, "exp"),
        P(None, "req", None, "exp"),
        P("req", None),
        P("req"),
        P("exp", None),
        P(),
        P(None, None, "exp"),
        P("exp", None),
        P(),
        P(("req", "exp"), None),
        P(("req", "exp"), None),
        P(("req", "exp"), None, None, None),
        P(("req", "exp"), None, None),
    )
    return jax.shard_map(
        on_device, mesh=mesh, in_specs=placed, out_specs=P(("req", "exp"), None), check_vma=False
    )
```
